256 devices in a mesh: ctx: 64 (over y, x, z_lo), mp: 4 (over z_hi, core).
Axes of the slice: x: 4, y: 4, z: 8 (z_hi: 2, z_lo: 4; z = z_hi * 4 + z_lo), core: 2. Of those that a mesh axis runs over, the one named last changes fastest.
Arguments:
- query_proj: bfloat16 [4096, 16384], P('mp', 'ctx'), may hold values from -6 to 6
- key_proj: bfloat16 [4096, 16384], P('mp', 'ctx'), may hold values from -6 to 6
- value_proj: bfloat16 [4096, 16384], P('mp', 'ctx'), may hold values from -6 to 6
- short_taps: float32 [3, 256, 7], P(None, 'mp'), may hold values from -2 to 2
- long_filter: float32 [4096, 16384], P(('mp', 'ctx')), may hold values from -0.046875 to 0.046875
- skip_bias: float32 [4096], P(('mp', 'ctx')), may hold values from -4 to 4
- out_weight: bfloat16 [4096, 4096], P('ctx', 'mp'), may hold values from -0.09375 to 0.09375
Outputs:
- mixed: bfloat16 [4096, 16384], P('mp', 'ctx')
The draws below stay inside these ranges and needn't reach their ends.
All inputs are finite; a program needn't handle non-finite values.
Results may differ from the reference program's by a relative error of at most 0.0064.
Values may be sent and summed in bfloat16 or wider, within the bound.
No kernel may reach another device: no remote copies, remote signals or barrier semaphores. Data moves between devices by JAX's collectives and lax.ppermute only.
A program may use at most 64 MiB of HBM per device.

```python
import jax
import jax.numpy as jnp
from jax import lax

D = 4096
FILTER_GROUPS = 256
KERNEL = 7
TOKENS = 16384


def block_levels(key, dims, split, least, largest):
    factor_of, own = 1.0, jax.random.fold_in(key, 6)
    for position, parts in split:
        heights = jnp.exp(jax.random.uniform(jax.random.fold_in(own, position), (parts,), jnp.float32, least / len(split), largest / len(split)))
        factor_of = factor_of * jnp.repeat(heights, dims[position] // parts).reshape([-1 if axis == position else 1 for axis in range(len(dims))])
    return factor_of


def noise(stream_key, shape, deviation, bound, shards=(), kind=jnp.bfloat16):
    result = deviation * jax.random.normal(stream_key, shape, jnp.float32)
    if shards:
        result = result * block_levels(stream_key, shape, shards, -0.22, 0.18)
    return jnp.clip(result, -bound, bound).astype(kind)


def setup_inputs(seed: int = 0) -> dict:
    splits = jax.random.split(jax.random.key(seed), 8)
    return {
        "query_proj": noise(splits[0], (D, TOKENS), 1.0, 6.0, ((0, 4), (1, 64))),
        "key_proj": noise(splits[1], (D, TOKENS), 1.0, 6.0, ((0, 4), (1, 64))),
        "value_proj": noise(splits[2], (D, TOKENS), 1.0, 6.0, ((0, 4), (1, 64))),
        "short_taps": noise(splits[3], (3, FILTER_GROUPS, KERNEL), KERNEL ** -0.5, 2.0, ((1, 4),), jnp.float32),
        "long_filter": noise(splits[4], (D, TOKENS), TOKENS ** -0.5, 0.046875, ((0, 256),), jnp.float32),
        "skip_bias": noise(splits[5], (D,), 1.0, 4.0, ((0, 256),), jnp.float32),
        "out_weight": noise(splits[6], (D, D), D ** -0.5, 0.09375, ((0, 64), (1, 4))),
    }


def causal_filter(signal, taps):
    padded = jnp.pad(signal.astype(jnp.float32), ((0, 0), (KERNEL - 1, 0)))
    running = jnp.zeros((signal.shape[0], TOKENS), jnp.float32)
    for shift_idx in range(KERNEL):
        start_col = KERNEL - 1 - shift_idx
        running = running + taps[:, shift_idx:shift_idx + 1] * padded[:, start_col:start_col + TOKENS]
    return running


def block_conv(pair):
    signal, filt = pair
    length = 2 * TOKENS
    spectrum = jnp.fft.rfft(signal, n=length, axis=1) * jnp.fft.rfft(filt, n=length, axis=1)
    return jnp.fft.irfft(spectrum, n=length, axis=1)[:, :TOKENS]


def reference(query_proj, key_proj, value_proj, short_taps, long_filter, skip_bias, out_weight):
    taps_all = jnp.repeat(short_taps.astype(jnp.float32), D // FILTER_GROUPS, axis=1)
    q_feat = causal_filter(query_proj, taps_all[0])
    k_feat = causal_filter(key_proj, taps_all[1])
    v_feat = causal_filter(value_proj, taps_all[2])
    product = (k_feat * v_feat).astype(jnp.bfloat16)
    product_f = product.astype(jnp.float32)
    rows_per = min(D, 512)
    signal_blocks = product_f.reshape(D // rows_per, rows_per, TOKENS)
    filter_blocks = long_filter.astype(jnp.float32).reshape(D // rows_per, rows_per, TOKENS)
    conv = lax.map(block_conv, (signal_blocks, filter_blocks)).reshape(D, TOKENS)
    mixed_chan = (conv + skip_bias[:, None] * product_f).astype(jnp.bfloat16)
    gated = (q_feat * mixed_chan.astype(jnp.float32)).astype(jnp.bfloat16)
    return jnp.dot(out_weight.T, gated, preferred_element_type=jnp.float32).astype(jnp.bfloat16)
```

```python
import math

import jax
import jax.numpy as jnp
import numpy as np
from jax import lax
from jax.experimental import pallas as pl
from jax.experimental.pallas import tpu as pltpu
from jax.sharding import Mesh, PartitionSpec as P

BF16 = jnp.bfloat16
F32 = jnp.float32
TAIL = 16
CTX = ("y", "x", "zl")
VMEM_LIMIT = 48 * 1024 * 1024


def hi_lo(table):
    hi = table.astype(np.float32).astype(jnp.bfloat16)
    lo = (table - hi.astype(np.float64)).astype(np.float32).astype(jnp.bfloat16)
    return hi, lo


def dft_tables(outer, inner):
    length = outer * inner
    freq = np.arange(outer)[:, None] + 0.25
    angle = 2.0 * np.pi * freq * np.arange(outer)[None, :] / outer
    first = np.concatenate([np.cos(angle), -np.sin(angle)], axis=0)
    spin = 2.0 * np.pi * freq * np.arange(inner)[None, :] / length
    steps = np.outer(np.arange(inner), np.arange(inner)) % inner
    turn = 2.0 * np.pi * steps / inner
    cos, sin = np.cos(turn), np.sin(turn)
    second = np.block([[cos, -sin], [sin, cos]])
    return {
        "first": hi_lo(first),
        "last": hi_lo(first.T.copy()),
        "spin": (np.cos(spin).astype(np.float32), np.sin(spin).astype(np.float32)),
        "second": hi_lo(second),
    }


def dot(left, right):
    return jnp.dot(left, right, preferred_element_type=F32)


def split_bf16(value):
    hi = value.astype(BF16)
    return hi, (value - hi.astype(F32)).astype(BF16)


def tail_kernel(q_ref, k_ref, v_ref, out_ref):
    lanes = q_ref.shape[1]
    row = lax.broadcasted_iota(jnp.int32, (TAIL, lanes), 0)
    lane = lax.broadcasted_iota(jnp.int32, (TAIL, lanes), 1)
    pick = jnp.where(lane == lanes - TAIL + row, 1.0, 0.0).astype(BF16)
    for index, ref in enumerate((q_ref, k_ref, v_ref)):
        picked = lax.dot_general(pick, ref[...], (((1,), (1,)), ((), ())), preferred_element_type=F32)
        out_ref[index] = picked.astype(BF16)


def take_tails(query, key, value):
    rows, cols = query.shape
    spec = pl.BlockSpec((rows, 128), lambda i: (0, cols // 128 - 1))
    return pl.pallas_call(
        tail_kernel,
        grid=(1,),
        in_specs=[spec] * 3,
        out_specs=pl.BlockSpec((3, TAIL, rows), lambda i: (0, 0, 0)),
        out_shape=jax.ShapeDtypeStruct((3, TAIL, rows), BF16),
        name="tails",
    )(query, key, value)


def short_kernel(taps_ref, q_ref, k_ref, v_ref, rim_ref, q_out, u_out, left_ref):
    rows, cols = q_ref.shape
    _, groups, taps = taps_ref.shape
    size = rows // groups
    row = lax.broadcasted_iota(jnp.int32, (TAIL, 128), 0)
    lane = lax.broadcasted_iota(jnp.int32, (TAIL, 128), 1)
    place = jnp.where(lane == 128 - TAIL + row, 1.0, 0.0).astype(BF16)
    for index in range(3):
        left_ref[index] = lax.dot_general(
            rim_ref[index], place, (((0,), (0,)), ((), ())), preferred_element_type=F32
        )
    lane = lax.broadcasted_iota(jnp.int32, (size, 128), 1)

    def group(g, carry):
        at = pl.ds(pl.multiple_of(g * size, size), size)
        feats = []
        for index, ref in enumerate((q_ref, k_ref, v_ref)):
            wide = ref[at, :].astype(F32)
            tiles = [left_ref[index, at, :]] + [wide[:, i * 128 : i * 128 + 128] for i in range(cols // 128)]
            sums = [taps_ref[index, g, 0] * tile for tile in tiles[1:]]
            for tap in range(1, taps):
                turned = [pltpu.roll(tile, tap, 1) for tile in tiles]
                weight = taps_ref[index, g, tap]
                for i in range(cols // 128):
                    sums[i] += weight * jnp.where(lane >= tap, turned[i + 1], turned[i])
            feats.append(sums)
        for i in range(cols // 128):
            q_out[at, i * 128 : i * 128 + 128] = feats[0][i].astype(BF16)
            u_out[at, i * 128 : i * 128 + 128] = (feats[1][i] * feats[2][i]).astype(BF16)
        return carry

    lax.fori_loop(0, groups, group, 0, unroll=2)


def short_filters(taps, query, key, value, rims):
    rows, cols = query.shape
    whole = pl.BlockSpec(memory_space=pltpu.VMEM)
    return pl.pallas_call(
        short_kernel,
        in_specs=[pl.BlockSpec(memory_space=pltpu.SMEM)] + [whole] * 4,
        out_specs=[whole] * 2,
        out_shape=[jax.ShapeDtypeStruct((rows, cols), BF16)] * 2,
        scratch_shapes=[pltpu.VMEM((3, rows, 128), F32)],
        compiler_params=pltpu.CompilerParams(vmem_limit_bytes=VMEM_LIMIT),
        cost_estimate=pl.CostEstimate(flops=3 * 14 * rows * cols, bytes_accessed=10 * rows * cols, transcendentals=0),
        name="short_filters",
    )(taps, query, key, value, rims)


def second_dft(hi, lo, second_hi, second_lo):
    return dot(hi, second_hi[...]) + dot(lo, second_hi[...]) + dot(hi, second_lo[...])


def channel_rows(ref, c, outer, chans):
    halves = ref.shape[0] // (outer * chans)
    parts = [ref[pl.ds(half * outer * chans + c, outer, stride=chans), :] for half in range(halves)]
    return jnp.concatenate(parts, axis=1)


def filter_kernel(scale, filt_ref, f_hi, f_lo, cos_ref, sin_ref, s_hi, s_lo, out_ref, rows_ref, g_hi, g_lo):
    chans, _ = filt_ref.shape
    outer, inner = cos_ref.shape
    for half in range(inner // 128):
        for a in range(outer):
            start = a * inner + half * 128
            at = (half * outer + a) * chans
            rows_ref[at : at + chans, :] = filt_ref[:, start : start + 128]

    def channel(c, carry):
        hi, lo = split_bf16(channel_rows(rows_ref, c, outer, chans) * scale)
        mixed = dot(f_hi[...], hi) + dot(f_hi[...], lo) + dot(f_lo[...], hi)
        re, im = mixed[:outer], mixed[outer:]
        at = pl.ds(pl.multiple_of(c * outer, outer), outer)
        g_hi[at, :inner], g_lo[at, :inner] = split_bf16(re * cos_ref[...] + im * sin_ref[...])
        g_hi[at, inner:], g_lo[at, inner:] = split_bf16(im * cos_ref[...] - re * sin_ref[...])
        return carry

    lax.fori_loop(0, chans, channel, 0, unroll=2)

    def block(i, carry):
        at = pl.ds(pl.multiple_of(i * 256, 256), 256)
        out_ref[at, :] = second_dft(g_hi[at, :], g_lo[at, :], s_hi, s_lo)
        return carry

    lax.fori_loop(0, chans * outer // 256, block, 0)


def filter_spectrum(long_filter, tables, outer, inner):
    chans = long_filter.shape[0]
    rows = chans * outer
    whole = pl.BlockSpec(memory_space=pltpu.VMEM)
    operands = (long_filter, *tables["first"], *tables["spin"], *tables["second"])
    return pl.pallas_call(
        lambda *refs: filter_kernel(1.0 / (outer * inner), *refs),
        in_specs=[whole] * len(operands),
        out_specs=whole,
        out_shape=jax.ShapeDtypeStruct((rows, 2 * inner), F32),
        scratch_shapes=[
            pltpu.VMEM((rows * inner // 128, 128), F32),
            pltpu.VMEM((rows, 2 * inner), BF16),
            pltpu.VMEM((rows, 2 * inner), BF16),
        ],
        compiler_params=pltpu.CompilerParams(vmem_limit_bytes=VMEM_LIMIT),
        cost_estimate=pl.CostEstimate(flops=3 * 2 * rows * 4 * inner * inner, bytes_accessed=5 * 2**20, transcendentals=0),
        name="filter_spectrum",
    )(*operands)


def conv_kernel(
    skip_ref, u_ref, spec_ref, f_hi, f_lo, l_hi, l_lo, cos_ref, sin_ref, s_hi, s_lo,
    out_ref, rows_ref, z_ref, g_hi, g_lo,
):
    outer, chans, inner = u_ref.shape
    rows = outer * chans
    halves = inner // 128
    flat = u_ref[...].reshape(rows, inner).astype(F32)
    for half in range(halves):
        rows_ref[half * rows : (half + 1) * rows, :] = flat[:, half * 128 : (half + 1) * 128]

    def channel(c, carry):
        sig = channel_rows(rows_ref, c, outer, chans).astype(BF16)
        mixed = dot(f_hi[...], sig) + dot(f_lo[...], sig)
        re, im = mixed[:outer], mixed[outer:]
        at = pl.ds(pl.multiple_of(c * outer, outer), outer)
        g_hi[at, :inner], g_lo[at, :inner] = split_bf16(re * cos_ref[...] + im * sin_ref[...])
        g_hi[at, inner:], g_lo[at, inner:] = split_bf16(im * cos_ref[...] - re * sin_ref[...])
        return carry

    lax.fori_loop(0, chans, channel, 0, unroll=2)

    def block(i, carry):
        at = pl.ds(pl.multiple_of(i * 256, 256), 256)
        sig = second_dft(g_hi[at, :], g_lo[at, :], s_hi, s_lo)
        sr, si = sig[:, :inner], sig[:, inner:]
        hr, hm = spec_ref[at, :inner], spec_ref[at, inner:]
        r_hi, r_lo = split_bf16(sr * hr - si * hm)
        i_hi, i_lo = split_bf16(-(sr * hm + si * hr))
        back = second_dft(
            jnp.concatenate([r_hi, i_hi], axis=1), jnp.concatenate([r_lo, i_lo], axis=1), s_hi, s_lo
        )
        back = back.reshape(256 // outer, outer, 2 * inner)
        re, im = back[:, :, :inner], back[:, :, inner:]
        cos, sin = cos_ref[...], sin_ref[...]
        r_hi, r_lo = split_bf16((re * cos + im * sin).reshape(256, inner))
        i_hi, i_lo = split_bf16((re * sin - im * cos).reshape(256, inner))
        g_hi[at, :inner], g_lo[at, :inner] = r_hi, r_lo
        g_hi[at, inner:], g_lo[at, inner:] = i_hi, i_lo
        return carry

    lax.fori_loop(0, chans * outer // 256, block, 0)

    def finish(c, carry):
        at = pl.ds(pl.multiple_of(c * outer, outer), outer)
        hi = jnp.concatenate([g_hi[at, :inner], g_hi[at, inner:]], axis=0)
        lo = jnp.concatenate([g_lo[at, :inner], g_lo[at, inner:]], axis=0)
        conv = dot(l_hi[...], hi) + dot(l_hi[...], lo) + dot(l_lo[...], hi)
        mixed = conv + skip_ref[c] * channel_rows(rows_ref, c, outer, chans)
        for half in range(halves):
            z_ref[pl.ds(half * rows + c, outer, stride=chans), :] = mixed[:, half * 128 : (half + 1) * 128]
        return carry

    lax.fori_loop(0, chans, finish, 0, unroll=2)
    for half in range(halves):
        result = z_ref[half * rows : (half + 1) * rows, :].astype(BF16).reshape(outer, chans, 128)
        for copy in range(out_ref.shape[1]):
            out_ref[:, copy, :, half * 128 : (half + 1) * 128] = result


def long_mix(chan_prod, spectrum, skip_bias, tables, copies):
    outer, chans, inner = chan_prod.shape
    rows = outer * chans
    whole = pl.BlockSpec(memory_space=pltpu.VMEM)
    operands = (chan_prod, spectrum, *tables["first"], *tables["last"], *tables["spin"], *tables["second"])
    return pl.pallas_call(
        conv_kernel,
        in_specs=[pl.BlockSpec(memory_space=pltpu.SMEM)] + [whole] * len(operands),
        out_specs=whole,
        out_shape=jax.ShapeDtypeStruct((outer, copies, chans, inner), BF16),
        scratch_shapes=[
            pltpu.VMEM((rows * inner // 128, 128), F32),
            pltpu.VMEM((rows * inner // 128, 128), F32),
            pltpu.VMEM((rows, 2 * inner), BF16),
            pltpu.VMEM((rows, 2 * inner), BF16),
        ],
        compiler_params=pltpu.CompilerParams(vmem_limit_bytes=VMEM_LIMIT),
        cost_estimate=pl.CostEstimate(flops=6 * 2 * rows * 4 * inner * inner, bytes_accessed=6 * 2**20, transcendentals=0),
        name="long_conv",
    )(skip_bias, *operands)


def project_kernel(place_ref, z_own, z_other, q_own, q_other, w_ref, out_ref, g_ref, gt_ref):
    ctx, halves, chans, cols = z_own.shape
    panel = ctx * chans
    unit = 4 * chans

    @pl.when(pl.program_id(0) == 0)
    def _():
        zl, zh, core = place_ref[0], place_ref[1], place_ref[2]
        for other, (z, q) in enumerate(((z_own, q_own), (z_other, q_other))):
            for half in range(halves):
                index = half * 2 + jnp.bitwise_xor(core, other)
                source = jnp.bitwise_xor(zh, half)
                for unit_at in range(ctx // 4):
                    z_part = z[unit_at * 4 : unit_at * 4 + 4, half].reshape(unit, cols).astype(F32)
                    q_part = q[source, unit_at * unit : (unit_at + 1) * unit, :].astype(F32)
                    turned = jnp.bitwise_and(zl - unit_at % 4, 3)
                    start = index * panel + (unit_at // 4) * 4 * unit + turned * unit
                    g_ref[pl.ds(pl.multiple_of(start, unit), unit), :] = (q_part * z_part).astype(BF16)
        for at in range(0, 4 * panel, 256):
            gt_ref[:, at : at + 256] = g_ref[at : at + 256, :].T

    out_ref[...] = dot(gt_ref[...], w_ref[...]).T.astype(BF16)


def project(place, z_own, z_other, q_own, q_other, weight):
    depth, width = weight.shape
    cols = z_own.shape[3]
    block = 256
    keep = lambda rank: (lambda i: (0,) * rank)
    return pl.pallas_call(
        project_kernel,
        grid=(width // block,),
        in_specs=[
            pl.BlockSpec(memory_space=pltpu.SMEM),
            pl.BlockSpec(z_own.shape, keep(4)),
            pl.BlockSpec(z_own.shape, keep(4)),
            pl.BlockSpec(q_own.shape, keep(3)),
            pl.BlockSpec(q_own.shape, keep(3)),
            pl.BlockSpec((depth, block), lambda i: (0, i)),
        ],
        out_specs=pl.BlockSpec((block, cols), lambda i: (i, 0)),
        out_shape=jax.ShapeDtypeStruct((width, cols), BF16),
        scratch_shapes=[pltpu.VMEM((depth, cols), BF16), pltpu.VMEM((cols, depth), BF16)],
        compiler_params=pltpu.CompilerParams(vmem_limit_bytes=VMEM_LIMIT),
        cost_estimate=pl.CostEstimate(flops=2 * depth * width * cols, bytes_accessed=2 * depth * (width + cols), transcendentals=0),
        name="project",
    )(place, z_own, z_other, q_own, q_other, weight)


def turned(value, axis, steps):
    count = lax.axis_size(axis)
    return lax.ppermute(value, axis, [(source, (source + steps) % count) for source in range(count)])


def shards(query_proj, key_proj, value_proj, short_taps, long_filter, skip_bias, out_weight):
    rows, cols = query_proj.shape
    ctx = lax.axis_size(CTX)
    chans = long_filter.shape[0]
    tables = dft_tables(ctx, cols)

    tails = take_tails(query_proj, key_proj, value_proj)
    rims = lax.ppermute(tails, CTX, [(source, source + 1) for source in range(ctx - 1)])

    weight_run = jnp.concatenate([out_weight] + [turned(out_weight, "zl", step) for step in (1, 2, 3)], axis=0)
    weight = lax.all_gather(weight_run, ("y", "x"), axis=0, tiled=True)

    spectrum = filter_spectrum(long_filter, tables, ctx, cols)
    q_feat, product = short_filters(short_taps, query_proj, key_proj, value_proj, rims)

    chan_prod = lax.all_to_all(product.reshape(ctx, chans, cols), CTX, split_axis=0, concat_axis=0, tiled=True)
    q_own = jnp.stack([q_feat, turned(q_feat, "zh", 1)])
    q_other = turned(q_own, "core", 1)

    mixed = long_mix(chan_prod, spectrum, skip_bias, tables, 2)
    z_own = lax.all_to_all(
        mixed.reshape(2 * ctx, chans, cols), CTX + ("zh",), split_axis=0, concat_axis=0, tiled=True
    ).reshape(ctx, 2, chans, cols)
    z_other = turned(z_own, "core", 1)

    place = jnp.stack([lax.axis_index(name) for name in ("zl", "zh", "core")]).astype(jnp.int32)
    return project(place, z_own, z_other, q_own, q_other, weight)


def solution(mesh):
    fine = Mesh(mesh.devices.reshape(4, 4, 4, 2, 2), ("y", "x", "zl", "zh", "core"))
    mp = ("zh", "core")
    return jax.shard_map(
        shards,
        mesh=fine,
        in_specs=(
            P(mp, CTX),
            P(mp, CTX),
            P(mp, CTX),
            P(None, mp, None),
            P(mp + CTX, None),
            P(mp + CTX),
            P(CTX, mp),
        ),
        out_specs=P(mp, CTX),
        check_vma=False,
    )
```

```python
import math

import jax
import jax.numpy as jnp
import numpy as np
from jax import lax
from jax.experimental import pallas as pl
from jax.experimental.pallas import tpu as pltpu
from jax.sharding import Mesh, PartitionSpec as P

BF16 = jnp.bfloat16
F32 = jnp.float32
CTX = ("y", "x", "zl")
VMEM_LIMIT = 60 * 1024 * 1024


def hi_lo(table):
    hi = table.astype(np.float32).astype(jnp.bfloat16)
    lo = (table - hi.astype(np.float64)).astype(np.float32).astype(jnp.bfloat16)
    return hi, lo


def dft_tables(outer, inner):
    length = outer * inner
    freq = np.arange(outer)[:, None] + 0.25
    angle = 2.0 * np.pi * freq * np.arange(outer)[None, :] / outer
    first = np.concatenate([np.cos(angle), -np.sin(angle)], axis=0)
    spin = 2.0 * np.pi * freq * np.arange(inner)[None, :] / length
    steps = np.outer(np.arange(inner), np.arange(inner)) % inner
    turn = 2.0 * np.pi * steps / inner
    cos, sin = np.cos(turn), np.sin(turn)
    second = np.block([[cos, -sin], [sin, cos]])
    return {
        "first": hi_lo(first),
        "last": hi_lo(first.T.copy()),
        "spin": (np.cos(spin).astype(np.float32), np.sin(spin).astype(np.float32)),
        "second": hi_lo(second),
    }


def dot(left, right):
    return jnp.dot(left, right, preferred_element_type=F32)


def split_bf16(value):
    hi = value.astype(BF16)
    return hi, (value - hi.astype(F32)).astype(BF16)


def lane_ids(rows):
    return lax.broadcasted_iota(jnp.int32, (rows, 128), 1)


def filter_tiles(weights, before, tiles, lane):
    turned = {}
    for tap in range(1, len(weights)):
        for index, tile in enumerate(tiles):
            turned[index, tap] = pltpu.roll(tile, tap, 1)
        turned[-1, tap] = 0.0 if before is None else pltpu.roll(before, tap, 1)
    sums = []
    for index, tile in enumerate(tiles):
        total = weights[0] * tile
        for tap in range(1, len(weights)):
            total += weights[tap] * jnp.where(lane >= tap, turned[index, tap], turned[index - 1, tap])
        sums.append(total)
    return sums


def short_kernel(taps_ref, q_ref, k_ref, v_ref, out_ref):
    rows, cols = q_ref.shape
    taps = taps_ref.shape[2]
    size = out_ref.shape[1]
    first = pl.program_id(0) * (rows // size)
    lane = lane_ids(size)
    for g in range(rows // size):
        at = pl.ds(g * size, size)
        feats, edges = [], []
        for index, ref in ((1, k_ref), (2, v_ref)):
            wide = ref[at, :].astype(F32)
            tiles = [wide[:, i * 128 : i * 128 + 128] for i in range(cols // 128)]
            weights = [taps_ref[index, first + g, tap] for tap in range(taps)]
            feats.append(filter_tiles(weights, None, tiles, lane))
            shift = 8 if index == 1 else 24
            edges += [pltpu.roll(tiles[-1], shift, 1), pltpu.roll(tiles[0], shift, 1)]
        for i in range(cols // 128):
            out_ref[g, :, i * 128 : i * 128 + 128] = (feats[0][i] * feats[1][i]).astype(BF16)
        out_ref[g, :, cols : 2 * cols] = q_ref[at, :]
        edge = jnp.where(lane < 16, jnp.where(lane < 8, edges[0], edges[1]), jnp.where(lane < 24, edges[2], edges[3]))
        out_ref[g, :, 2 * cols :] = edge.astype(BF16)


def short_filters(taps, query, key, value, ctx, blocks=4):
    rows, cols = query.shape
    size = rows // ctx
    spec = pl.BlockSpec((rows // blocks, cols), lambda i: (i, 0))
    return pl.pallas_call(
        short_kernel,
        grid=(blocks,),
        in_specs=[pl.BlockSpec(memory_space=pltpu.SMEM)] + [spec] * 3,
        out_specs=pl.BlockSpec((ctx // blocks, size, 2 * cols + 128), lambda i: (i, 0, 0)),
        out_shape=jax.ShapeDtypeStruct((ctx, size, 2 * cols + 128), BF16),
        compiler_params=pltpu.CompilerParams(vmem_limit_bytes=VMEM_LIMIT),
        cost_estimate=pl.CostEstimate(flops=2 * 14 * rows * cols, bytes_accessed=10 * rows * cols, transcendentals=0),
        name="short_filters",
    )(taps, query, key, value)


def second_dft(hi, lo, second_hi, second_lo):
    return dot(hi, second_hi[...]) + dot(lo, second_hi[...]) + dot(hi, second_lo[...])


def channel_rows(ref, c, outer, chans):
    halves = ref.shape[0] // (outer * chans)
    parts = [ref[pl.ds(half * outer * chans + c, outer, stride=chans), :] for half in range(halves)]
    return jnp.concatenate(parts, axis=1)


def filter_kernel(scale, filt_ref, f_hi, f_lo, cos_ref, sin_ref, s_hi, s_lo, out_ref, rows_ref, g_hi, g_lo):
    chans, _ = filt_ref.shape
    outer, inner = cos_ref.shape
    for half in range(inner // 128):
        for a in range(outer):
            start = a * inner + half * 128
            at = (half * outer + a) * chans
            rows_ref[at : at + chans, :] = filt_ref[:, start : start + 128]

    for c in range(chans):
        hi, lo = split_bf16(channel_rows(rows_ref, c, outer, chans) * scale)
        mixed = dot(f_hi[...], hi) + dot(f_hi[...], lo) + dot(f_lo[...], hi)
        re, im = mixed[:outer], mixed[outer:]
        at = pl.ds(c * outer, outer)
        g_hi[at, :inner], g_lo[at, :inner] = split_bf16(re * cos_ref[...] + im * sin_ref[...])
        g_hi[at, inner:], g_lo[at, inner:] = split_bf16(im * cos_ref[...] - re * sin_ref[...])

    for i in range(chans * outer // 256):
        at = pl.ds(i * 256, 256)
        out_ref[at, :] = second_dft(g_hi[at, :], g_lo[at, :], s_hi, s_lo)


def filter_spectrum(long_filter, tables, outer, inner):
    chans = long_filter.shape[0]
    rows = chans * outer
    whole = lambda shape: pl.BlockSpec(shape, lambda i: (0,) * len(shape))
    operands = (long_filter, *tables["first"], *tables["spin"], *tables["second"])
    return pl.pallas_call(
        lambda *refs: filter_kernel(1.0 / (outer * inner), *refs),
        grid=(1,),
        in_specs=[whole(operand.shape) for operand in operands],
        out_specs=whole((rows, 2 * inner)),
        out_shape=jax.ShapeDtypeStruct((rows, 2 * inner), F32),
        scratch_shapes=[
            pltpu.VMEM((rows * inner // 128, 128), F32),
            pltpu.VMEM((rows, 2 * inner), BF16),
            pltpu.VMEM((rows, 2 * inner), BF16),
        ],
        compiler_params=pltpu.CompilerParams(vmem_limit_bytes=VMEM_LIMIT),
        cost_estimate=pl.CostEstimate(flops=3 * 2 * rows * 4 * inner * inner, bytes_accessed=5 * 2**20, transcendentals=0),
        name="filter_spectrum",
    )(*operands)


def conv_kernel(
    skip_ref, taps_ref, in_ref, f_hi, f_lo, l_hi, l_lo, cos_ref, sin_ref, spec_hbm, s_hi_hbm, s_lo_hbm,
    out_ref, rows_ref, z_ref, q_ref, edge_ref, g_hi, g_lo, spec_ref, s_hi, s_lo, sems,
):
    fetches = [
        pltpu.make_async_copy(source, target, sems.at[index])
        for index, (source, target) in enumerate(((spec_hbm, spec_ref), (s_hi_hbm, s_hi), (s_lo_hbm, s_lo)))
    ]
    for fetch in fetches:
        fetch.start()
    outer, chans, width = in_ref.shape
    inner = (width - 128) // 2
    halves = inner // 128
    rows = outer * chans
    taps = taps_ref.shape[1]
    blocks = 8
    step = rows // blocks
    units = outer // blocks
    lane = lane_ids(step)

    edge_ref[:chans, :] = jnp.zeros((chans, 128), F32)
    q_ref[(halves - 1) * (rows + chans) : (halves - 1) * (rows + chans) + chans, :] = jnp.zeros((chans, 128), F32)
    edge_ref[chans:, :] = in_ref[:, :, 2 * inner :].reshape(rows, 128).astype(F32)
    for half in range(halves):
        at = half * (rows + chans) + chans
        q_ref[at : at + rows, :] = (
            in_ref[:, :, inner + half * 128 : inner + half * 128 + 128].reshape(rows, 128).astype(F32)
        )

    weights = [jnp.where(lane < 16, taps_ref[1, tap], taps_ref[2, tap]) for tap in range(taps)]

    for i in range(blocks):
        at = i * step
        edge = jnp.where(jnp.bitwise_and(lane, 8) == 0, edge_ref[at : at + step, :], edge_ref[at + chans : at + chans + step, :])
        total = weights[0] * edge
        for tap in range(1, taps):
            total += weights[tap] * pltpu.roll(edge, tap, 1)
        first = (pltpu.roll(total, 120, 1) * pltpu.roll(total, 104, 1)).astype(BF16).astype(F32)
        sig = in_ref[i * units : (i + 1) * units, :, :inner].reshape(step, inner).astype(F32)
        rows_ref[at : at + step, :] = jnp.where(lane < taps - 1, first, sig[:, :128])
        for half in range(1, halves):
            rows_ref[half * rows + at : half * rows + at + step, :] = sig[:, half * 128 : half * 128 + 128]

    for c in range(chans):
        sig = channel_rows(rows_ref, c, outer, chans).astype(BF16)
        mixed = dot(f_hi[...], sig) + dot(f_lo[...], sig)
        re, im = mixed[:outer], mixed[outer:]
        at = pl.ds(c * outer, outer)
        g_hi[at, :inner], g_lo[at, :inner] = split_bf16(re * cos_ref[...] + im * sin_ref[...])
        g_hi[at, inner:], g_lo[at, inner:] = split_bf16(im * cos_ref[...] - re * sin_ref[...])

    for fetch in fetches:
        fetch.wait()

    for i in range(chans * outer // 256):
        at = pl.ds(i * 256, 256)
        sig = second_dft(g_hi[at, :], g_lo[at, :], s_hi, s_lo)
        sr, si = sig[:, :inner], sig[:, inner:]
        hr, hm = spec_ref[at, :inner], spec_ref[at, inner:]
        r_hi, r_lo = split_bf16(sr * hr - si * hm)
        i_hi, i_lo = split_bf16(-(sr * hm + si * hr))
        back = second_dft(
            jnp.concatenate([r_hi, i_hi], axis=1), jnp.concatenate([r_lo, i_lo], axis=1), s_hi, s_lo
        )
        back = back.reshape(256 // outer, outer, 2 * inner)
        re, im = back[:, :, :inner], back[:, :, inner:]
        cos, sin = cos_ref[...], sin_ref[...]
        r_hi, r_lo = split_bf16((re * cos + im * sin).reshape(256, inner))
        i_hi, i_lo = split_bf16((re * sin - im * cos).reshape(256, inner))
        for j in range(256 // outer):
            c = i * (256 // outer) + j
            part = slice(j * outer, (j + 1) * outer)
            hi = jnp.concatenate([r_hi[part], i_hi[part]], axis=0)
            lo = jnp.concatenate([r_lo[part], i_lo[part]], axis=0)
            conv = dot(l_hi[...], hi) + dot(l_hi[...], lo) + dot(l_lo[...], hi)
            mixed = conv + skip_ref[c] * channel_rows(rows_ref, c, outer, chans)
            for half in range(halves):
                z_ref[pl.ds(half * rows + c, outer, stride=chans), :] = mixed[:, half * 128 : (half + 1) * 128]

    q_taps = [taps_ref[0, tap] for tap in range(taps)]
    for i in range(blocks):
        at = i * step
        starts = [half * (rows + chans) + chans + at for half in range(halves)]
        tiles = [q_ref[start : start + step, :] for start in starts]
        start = (halves - 1) * (rows + chans) + at
        feats = filter_tiles(q_taps, q_ref[start : start + step, :], tiles, lane)
        for half in range(halves):
            mixed = z_ref[half * rows + at : half * rows + at + step, :].astype(BF16).astype(F32)
            result = (feats[half] * mixed).astype(BF16).reshape(units, chans, 128)
            for copy in range(out_ref.shape[1]):
                out_ref[i * units : (i + 1) * units, copy, :, half * 128 : (half + 1) * 128] = result


def long_mix(arrived, spectrum, skip_bias, taps, tables, copies):
    outer, chans, width = arrived.shape
    inner = (width - 128) // 2
    rows = outer * chans
    whole = lambda shape: pl.BlockSpec(shape, lambda i: (0,) * len(shape))
    scalars = pl.BlockSpec(memory_space=pltpu.SMEM)
    operands = (arrived, *tables["first"], *tables["last"], *tables["spin"])
    fetched = (spectrum, *tables["second"])
    return pl.pallas_call(
        conv_kernel,
        grid=(1,),
        in_specs=[scalars] * 2
        + [whole(operand.shape) for operand in operands]
        + [pl.BlockSpec(memory_space=pl.ANY)] * len(fetched),
        out_specs=whole((outer, copies, chans, inner)),
        out_shape=jax.ShapeDtypeStruct((outer, copies, chans, inner), BF16),
        scratch_shapes=[
            pltpu.VMEM((rows * inner // 128, 128), F32),
            pltpu.VMEM((rows * inner // 128, 128), F32),
            pltpu.VMEM(((rows + chans) * inner // 128, 128), F32),
            pltpu.VMEM((rows + chans, 128), F32),
            pltpu.VMEM((rows, 2 * inner), BF16),
            pltpu.VMEM((rows, 2 * inner), BF16),
            pltpu.VMEM((rows, 2 * inner), F32),
            pltpu.VMEM((2 * inner, 2 * inner), BF16),
            pltpu.VMEM((2 * inner, 2 * inner), BF16),
            pltpu.SemaphoreType.DMA((3,)),
        ],
        compiler_params=pltpu.CompilerParams(vmem_limit_bytes=VMEM_LIMIT),
        cost_estimate=pl.CostEstimate(flops=6 * 2 * rows * 4 * inner * inner, bytes_accessed=6 * 2**20, transcendentals=0),
        name="long_conv",
    )(skip_bias, taps, *operands, *fetched)


def project_kernel(last, place_ref, *refs):
    (z_ref, w_ref, sum_ref, out_ref, acc_ref) = refs if last else (refs[0], refs[1], None, refs[2], None)
    total_ref = acc_ref if last else out_ref
    _, _, chans, cols = z_ref.shape
    unit = 4 * chans
    step = pl.program_id(0)
    zl = place_ref[0]
    half = step // 2
    parts = []
    for x in range(2):
        for turn in range(4):
            start = (2 * (step % 2) + x) * 16 + 4 * jnp.bitwise_and(zl - turn, 3)
            parts.append(z_ref[pl.ds(start, 4), half].reshape(unit, cols))
    gated = jnp.concatenate(parts, axis=0)
    part = dot(gated.T, w_ref[...])

    @pl.when(step == 0)
    def _():
        total_ref[...] = part + sum_ref[...] if last else part

    @pl.when(step > 0)
    def _():
        total_ref[...] += part

    if last:
        @pl.when(step == pl.num_programs(0) - 1)
        def _():
            out_ref[...] = total_ref[...].T.astype(BF16)


def project(place, gated, weight, partial=None):
    depth, width = weight.shape
    cols = gated.shape[3]
    last = partial is not None
    block = depth // 8
    whole = lambda shape: pl.BlockSpec(shape, lambda i, place: (0,) * len(shape))
    in_specs = [whole(gated.shape), pl.BlockSpec((block, width), lambda i, place: (4 * (i // 2) + 2 * place[1] + i % 2, 0))]
    operands = [gated, weight]
    if last:
        in_specs.append(whole(partial.shape))
        operands.append(partial)
    return pl.pallas_call(
        lambda *refs: project_kernel(last, *refs),
        grid_spec=pltpu.PrefetchScalarGridSpec(
            num_scalar_prefetch=1,
            grid=(4,),
            in_specs=in_specs,
            out_specs=whole((width, cols) if last else (cols, width)),
            scratch_shapes=[pltpu.VMEM((cols, width), F32)] if last else [],
        ),
        out_shape=jax.ShapeDtypeStruct((width, cols), BF16) if last else jax.ShapeDtypeStruct((cols, width), F32),
        compiler_params=pltpu.CompilerParams(vmem_limit_bytes=VMEM_LIMIT),
        cost_estimate=pl.CostEstimate(flops=depth * width * cols, bytes_accessed=depth * width, transcendentals=0),
        name="project_last" if last else "project_first",
    )(place, *operands)


def turned(value, axis, steps):
    count = lax.axis_size(axis)
    return lax.ppermute(value, axis, [(source, (source + steps) % count) for source in range(count)])


def shards(query_proj, key_proj, value_proj, short_taps, long_filter, skip_bias, out_weight):
    rows, cols = query_proj.shape
    ctx = lax.axis_size(CTX)
    chans = long_filter.shape[0]
    tables = dft_tables(ctx, cols)

    pieces = [turned(out_weight, "zl", step) for step in (1, 2, 3)]
    ready = short_filters(short_taps, query_proj, key_proj, value_proj, ctx)
    ready, *pieces = lax.optimization_barrier((ready, *pieces))
    weight_run = jnp.concatenate([out_weight, *pieces], axis=0)
    weight = lax.all_gather(weight_run, ("y", "x"), axis=0, tiled=True)

    spectrum = filter_spectrum(long_filter, tables, ctx, cols)
    arrived = lax.all_to_all(ready, CTX, split_axis=0, concat_axis=0, tiled=True)
    own_taps = lax.dynamic_index_in_dim(short_taps, lax.axis_index(CTX), 1, keepdims=False)

    gated = long_mix(arrived, spectrum, skip_bias, own_taps, tables, 2)
    own = lax.all_to_all(
        gated.reshape(2 * ctx, chans, cols), CTX + ("zh",), split_axis=0, concat_axis=0, tiled=True
    ).reshape(ctx, 2, chans, cols)
    other = turned(own, "core", 1)

    zl, core = lax.axis_index("zl"), lax.axis_index("core")
    partial = project(jnp.stack([zl, core]).astype(jnp.int32), own, weight)
    return project(jnp.stack([zl, 1 - core]).astype(jnp.int32), other, weight, partial)


def solution(mesh):
    fine = Mesh(mesh.devices.reshape(4, 4, 4, 2, 2), ("y", "x", "zl", "zh", "core"))
    mp = ("zh", "core")
    return jax.shard_map(
        shards,
        mesh=fine,
        in_specs=(
            P(mp, CTX),
            P(mp, CTX),
            P(mp, CTX),
            P(None, mp, None),
            P(mp + CTX, None),
            P(mp + CTX),
            P(CTX, mp),
        ),
        out_specs=P(mp, CTX),
        check_vma=False,
    )
```

```python
import math

import jax
import jax.numpy as jnp
import numpy as np
from jax import lax
from jax.experimental import pallas as pl
from jax.experimental.pallas import tpu as pltpu
from jax.sharding import Mesh, PartitionSpec as P

BF16 = jnp.bfloat16
F32 = jnp.float32
CTX = ("y", "x", "zl")
VMEM_LIMIT = 60 * 1024 * 1024


def hi_lo(table):
    hi = table.astype(np.float32).astype(jnp.bfloat16)
    lo = (table - hi.astype(np.float64)).astype(np.float32).astype(jnp.bfloat16)
    return hi, lo


def dft_tables(outer, inner):
    length = outer * inner
    freq = np.arange(outer)[:, None] + 0.25
    angle = 2.0 * np.pi * freq * np.arange(outer)[None, :] / outer
    first = np.concatenate([np.cos(angle), -np.sin(angle)], axis=0)
    spin = 2.0 * np.pi * freq * np.arange(inner)[None, :] / length
    steps = np.outer(np.arange(inner), np.arange(inner)) % inner
    turn = 2.0 * np.pi * steps / inner
    cos, sin = np.cos(turn), np.sin(turn)
    second = np.block([[cos, -sin], [sin, cos]])
    return {
        "first": hi_lo(first),
        "last": hi_lo(first.T.copy()),
        "spin": (np.cos(spin).astype(np.float32), np.sin(spin).astype(np.float32)),
        "second": hi_lo(second),
    }


def dot(left, right):
    return jnp.dot(left, right, preferred_element_type=F32)


def split_bf16(value):
    hi = value.astype(BF16)
    return hi, (value - hi.astype(F32)).astype(BF16)


def lane_ids(rows):
    return lax.broadcasted_iota(jnp.int32, (rows, 128), 1)


def filter_tiles(weights, before, tiles, lane):
    turned = {}
    for tap in range(1, len(weights)):
        for index, tile in enumerate(tiles):
            turned[index, tap] = pltpu.roll(tile, tap, 1)
        turned[-1, tap] = 0.0 if before is None else pltpu.roll(before, tap, 1)
    sums = []
    for index, tile in enumerate(tiles):
        total = weights[0] * tile
        for tap in range(1, len(weights)):
            total += weights[tap] * jnp.where(lane >= tap, turned[index, tap], turned[index - 1, tap])
        sums.append(total)
    return sums


def short_kernel(taps_ref, k_ref, v_ref, out_ref):
    rows, cols = k_ref.shape
    taps = taps_ref.shape[1]
    size = out_ref.shape[1]
    first = pl.program_id(0) * (rows // size)
    lane = lane_ids(size)
    for g in range(rows // size):
        at = pl.ds(g * size, size)
        feats, edges = [], []
        for index, ref in ((1, k_ref), (2, v_ref)):
            wide = ref[at, :].astype(F32)
            tiles = [wide[:, i * 128 : i * 128 + 128] for i in range(cols // 128)]
            weights = [taps_ref[index, tap, first + g] for tap in range(taps)]
            feats.append(filter_tiles(weights, None, tiles, lane))
            shift = 8 if index == 1 else 24
            edges += [pltpu.roll(tiles[-1], shift, 1), pltpu.roll(tiles[0], shift, 1)]
        for i in range(cols // 128):
            out_ref[g, :, i * 128 : i * 128 + 128] = (feats[0][i] * feats[1][i]).astype(BF16)
        edge = jnp.where(lane < 16, jnp.where(lane < 8, edges[0], edges[1]), jnp.where(lane < 24, edges[2], edges[3]))
        out_ref[g, :, cols:] = edge.astype(BF16)


def short_filters(taps, key, value, ctx, blocks=4):
    rows, cols = key.shape
    size = rows // ctx
    spec = pl.BlockSpec((rows // blocks, cols), lambda i: (i, 0))
    return pl.pallas_call(
        short_kernel,
        grid=(blocks,),
        in_specs=[pl.BlockSpec(memory_space=pltpu.SMEM)] + [spec] * 2,
        out_specs=pl.BlockSpec((ctx // blocks, size, cols + 128), lambda i: (i, 0, 0)),
        out_shape=jax.ShapeDtypeStruct((ctx, size, cols + 128), BF16),
        compiler_params=pltpu.CompilerParams(vmem_limit_bytes=VMEM_LIMIT),
        cost_estimate=pl.CostEstimate(flops=2 * 14 * rows * cols, bytes_accessed=10 * rows * cols, transcendentals=0),
        name="short_filters",
    )(taps, key, value)


def tail_kernel(q_ref, out_ref):
    tail, rows = out_ref.shape
    row = lax.broadcasted_iota(jnp.int32, (tail, 128), 0)
    lane = lax.broadcasted_iota(jnp.int32, (tail, 128), 1)
    pick = jnp.where(lane == 128 - tail + row, 1.0, 0.0).astype(BF16)
    picked = lax.dot_general(pick, q_ref[...], (((1,), (1,)), ((), ())), preferred_element_type=F32)
    out_ref[...] = picked.astype(BF16)


def take_tail(query, tail=16):
    rows, cols = query.shape
    return pl.pallas_call(
        tail_kernel,
        grid=(1,),
        in_specs=[pl.BlockSpec((rows, 128), lambda i: (0, cols // 128 - 1))],
        out_specs=pl.BlockSpec((tail, rows), lambda i: (0, 0)),
        out_shape=jax.ShapeDtypeStruct((tail, rows), BF16),
        compiler_params=pltpu.CompilerParams(vmem_limit_bytes=VMEM_LIMIT),
        name="query_tail",
    )(query)


def query_kernel(taps_ref, q_ref, rim_ref, out_ref, left_ref):
    rows, cols = q_ref.shape
    taps = taps_ref.shape[1]
    tail = rim_ref.shape[0]
    groups = taps_ref.shape[2] // pl.num_programs(0)
    size = rows // groups
    first = pl.program_id(0) * groups
    row = lax.broadcasted_iota(jnp.int32, (tail, 128), 0)
    column = lax.broadcasted_iota(jnp.int32, (tail, 128), 1)
    place = jnp.where(column == 128 - tail + row, 1.0, 0.0).astype(BF16)
    left_ref[...] = lax.dot_general(rim_ref[...], place, (((0,), (0,)), ((), ())), preferred_element_type=F32)
    lane = lane_ids(size)
    for g in range(groups):
        at = pl.ds(g * size, size)
        wide = q_ref[at, :].astype(F32)
        tiles = [wide[:, i * 128 : i * 128 + 128] for i in range(cols // 128)]
        weights = [taps_ref[0, tap, first + g] for tap in range(taps)]
        for i, feat in enumerate(filter_tiles(weights, left_ref[at, :], tiles, lane)):
            out_ref[at, i * 128 : i * 128 + 128] = feat.astype(BF16)


def query_filter(taps, query, rim, blocks=4):
    rows, cols = query.shape
    spec = pl.BlockSpec((rows // blocks, cols), lambda i: (i, 0))
    return pl.pallas_call(
        query_kernel,
        grid=(blocks,),
        in_specs=[
            pl.BlockSpec(memory_space=pltpu.SMEM),
            spec,
            pl.BlockSpec((rim.shape[0], rows // blocks), lambda i: (0, i)),
        ],
        out_specs=spec,
        out_shape=jax.ShapeDtypeStruct((rows, cols), BF16),
        scratch_shapes=[pltpu.VMEM((rows // blocks, 128), F32)],
        compiler_params=pltpu.CompilerParams(vmem_limit_bytes=VMEM_LIMIT),
        name="query_filter",
    )(taps, query, rim)


def second_dft(hi, lo, second_hi, second_lo):
    return dot(hi, second_hi[...]) + dot(lo, second_hi[...]) + dot(hi, second_lo[...])


def channel_rows(ref, c, outer, chans):
    halves = ref.shape[0] // (outer * chans)
    parts = [ref[pl.ds(half * outer * chans + c, outer, stride=chans), :] for half in range(halves)]
    return jnp.concatenate(parts, axis=1)


def filter_kernel(scale, filt_ref, f_hi, f_lo, cos_ref, sin_ref, s_hi, s_lo, out_ref, rows_ref, g_hi, g_lo):
    chans, _ = filt_ref.shape
    outer, inner = cos_ref.shape
    for half in range(inner // 128):
        for a in range(outer):
            start = a * inner + half * 128
            at = (half * outer + a) * chans
            rows_ref[at : at + chans, :] = filt_ref[:, start : start + 128]

    for c in range(chans):
        hi, lo = split_bf16(channel_rows(rows_ref, c, outer, chans) * scale)
        mixed = dot(f_hi[...], hi) + dot(f_hi[...], lo) + dot(f_lo[...], hi)
        re, im = mixed[:outer], mixed[outer:]
        at = pl.ds(c * outer, outer)
        g_hi[at, :inner], g_lo[at, :inner] = split_bf16(re * cos_ref[...] + im * sin_ref[...])
        g_hi[at, inner:], g_lo[at, inner:] = split_bf16(im * cos_ref[...] - re * sin_ref[...])

    for i in range(chans * outer // 256):
        at = pl.ds(i * 256, 256)
        out_ref[at, :] = second_dft(g_hi[at, :], g_lo[at, :], s_hi, s_lo)


def filter_spectrum(long_filter, tables, outer, inner):
    chans = long_filter.shape[0]
    rows = chans * outer
    whole = lambda shape: pl.BlockSpec(shape, lambda i: (0,) * len(shape))
    operands = (long_filter, *tables["first"], *tables["spin"], *tables["second"])
    return pl.pallas_call(
        lambda *refs: filter_kernel(1.0 / (outer * inner), *refs),
        grid=(1,),
        in_specs=[whole(operand.shape) for operand in operands],
        out_specs=whole((rows, 2 * inner)),
        out_shape=jax.ShapeDtypeStruct((rows, 2 * inner), F32),
        scratch_shapes=[
            pltpu.VMEM((rows * inner // 128, 128), F32),
            pltpu.VMEM((rows, 2 * inner), BF16),
            pltpu.VMEM((rows, 2 * inner), BF16),
        ],
        compiler_params=pltpu.CompilerParams(vmem_limit_bytes=VMEM_LIMIT),
        cost_estimate=pl.CostEstimate(flops=2**20, bytes_accessed=2**20, transcendentals=0),
        name="filter_spectrum",
    )(*operands)


def conv_kernel(
    place_ref, skip_ref, taps_ref, in_ref, f_hi, f_lo, l_hi, l_lo, cos_ref, sin_ref, spec_hbm, s_hi_hbm, s_lo_hbm,
    out_ref, rows_ref, z_ref, edge_ref, g_hi, g_lo, spec_ref, s_hi, s_lo, sems,
):
    fetches = [
        pltpu.make_async_copy(source, target, sems.at[index])
        for index, (source, target) in enumerate(((spec_hbm, spec_ref), (s_hi_hbm, s_hi), (s_lo_hbm, s_lo)))
    ]
    for fetch in fetches:
        fetch.start()
    outer, chans, width = in_ref.shape
    inner = width - 128
    halves = inner // 128
    rows = outer * chans
    taps = taps_ref.shape[1]
    group = place_ref[0]
    blocks = 8
    step = rows // blocks
    units = outer // blocks
    lane = lane_ids(step)

    edge_ref[:chans, :] = jnp.zeros((chans, 128), F32)
    edge_ref[chans:, :] = in_ref[:, :, inner:].reshape(rows, 128).astype(F32)
    weights = [jnp.where(lane < 16, taps_ref[1, tap, group], taps_ref[2, tap, group]) for tap in range(taps)]

    for i in range(blocks):
        at = i * step
        edge = jnp.where(jnp.bitwise_and(lane, 8) == 0, edge_ref[at : at + step, :], edge_ref[at + chans : at + chans + step, :])
        total = weights[0] * edge
        for tap in range(1, taps):
            total += weights[tap] * pltpu.roll(edge, tap, 1)
        first = (pltpu.roll(total, 120, 1) * pltpu.roll(total, 104, 1)).astype(BF16).astype(F32)
        sig = in_ref[i * units : (i + 1) * units, :, :inner].reshape(step, inner).astype(F32)
        rows_ref[at : at + step, :] = jnp.where(lane < taps - 1, first, sig[:, :128])
        for half in range(1, halves):
            rows_ref[half * rows + at : half * rows + at + step, :] = sig[:, half * 128 : half * 128 + 128]

    for c in range(chans):
        sig = channel_rows(rows_ref, c, outer, chans).astype(BF16)
        mixed = dot(f_hi[...], sig) + dot(f_lo[...], sig)
        re, im = mixed[:outer], mixed[outer:]
        at = pl.ds(c * outer, outer)
        g_hi[at, :inner], g_lo[at, :inner] = split_bf16(re * cos_ref[...] + im * sin_ref[...])
        g_hi[at, inner:], g_lo[at, inner:] = split_bf16(im * cos_ref[...] - re * sin_ref[...])

    for fetch in fetches:
        fetch.wait()

    for i in range(chans * outer // 256):
        at = pl.ds(i * 256, 256)
        sig = second_dft(g_hi[at, :], g_lo[at, :], s_hi, s_lo)
        sr, si = sig[:, :inner], sig[:, inner:]
        hr, hm = spec_ref[at, :inner], spec_ref[at, inner:]
        r_hi, r_lo = split_bf16(sr * hr - si * hm)
        i_hi, i_lo = split_bf16(-(sr * hm + si * hr))
        back = second_dft(
            jnp.concatenate([r_hi, i_hi], axis=1), jnp.concatenate([r_lo, i_lo], axis=1), s_hi, s_lo
        )
        back = back.reshape(256 // outer, outer, 2 * inner)
        re, im = back[:, :, :inner], back[:, :, inner:]
        cos, sin = cos_ref[...], sin_ref[...]
        r_hi, r_lo = split_bf16((re * cos + im * sin).reshape(256, inner))
        i_hi, i_lo = split_bf16((re * sin - im * cos).reshape(256, inner))
        for j in range(256 // outer):
            c = i * (256 // outer) + j
            part = slice(j * outer, (j + 1) * outer)
            hi = jnp.concatenate([r_hi[part], i_hi[part]], axis=0)
            lo = jnp.concatenate([r_lo[part], i_lo[part]], axis=0)
            conv = dot(l_hi[...], hi) + dot(l_hi[...], lo) + dot(l_lo[...], hi)
            mixed = conv + skip_ref[c] * channel_rows(rows_ref, c, outer, chans)
            for half in range(halves):
                z_ref[pl.ds(half * rows + c, outer, stride=chans), :] = mixed[:, half * 128 : (half + 1) * 128]

    for half in range(halves):
        result = z_ref[half * rows : (half + 1) * rows, :].astype(BF16).reshape(outer, chans, 128)
        for copy in range(out_ref.shape[1]):
            out_ref[:, copy, :, half * 128 : (half + 1) * 128] = result


def long_mix(place, arrived, spectrum, skip_bias, taps, tables, copies):
    outer, chans, width = arrived.shape
    inner = width - 128
    rows = outer * chans
    whole = lambda shape: pl.BlockSpec(shape, lambda i: (0,) * len(shape))
    scalars = pl.BlockSpec(memory_space=pltpu.SMEM)
    operands = (arrived, *tables["first"], *tables["last"], *tables["spin"])
    fetched = (spectrum, *tables["second"])
    return pl.pallas_call(
        conv_kernel,
        grid=(1,),
        in_specs=[scalars] * 3
        + [whole(operand.shape) for operand in operands]
        + [pl.BlockSpec(memory_space=pl.ANY)] * len(fetched),
        out_specs=whole((outer, copies, chans, inner)),
        out_shape=jax.ShapeDtypeStruct((outer, copies, chans, inner), BF16),
        scratch_shapes=[
            pltpu.VMEM((rows * inner // 128, 128), F32),
            pltpu.VMEM((rows * inner // 128, 128), F32),
            pltpu.VMEM((rows + chans, 128), F32),
            pltpu.VMEM((rows, 2 * inner), BF16),
            pltpu.VMEM((rows, 2 * inner), BF16),
            pltpu.VMEM((rows, 2 * inner), F32),
            pltpu.VMEM((2 * inner, 2 * inner), BF16),
            pltpu.VMEM((2 * inner, 2 * inner), BF16),
            pltpu.SemaphoreType.DMA((3,)),
        ],
        compiler_params=pltpu.CompilerParams(vmem_limit_bytes=VMEM_LIMIT),
        cost_estimate=pl.CostEstimate(flops=2**20, bytes_accessed=2**20, transcendentals=0),
        name="long_conv",
    )(place, skip_bias, taps, *operands, *fetched)


def gate_kernel(place_ref, z_ref, q_own, q_far, out_ref):
    _, halves, chans, cols = z_ref.shape
    unit = 4 * chans
    zl, zh = place_ref[1], place_ref[2]
    for half in range(halves):
        for x in range(4):
            parts = []
            for turn in range(4):
                start = x * 4 + jnp.bitwise_and(zl - turn, 3)
                at = pl.ds(pl.multiple_of(start * unit, unit), unit)
                feat = jnp.where(zh == half, q_own[at, :].astype(F32), q_far[at, :].astype(F32))
                mixed = z_ref[pl.ds(start * 4, 4), half].reshape(unit, cols).astype(F32)
                parts.append((feat * mixed).astype(BF16))
            to = (half * 4 + x) * 4 * unit
            out_ref[:, to : to + 4 * unit] = jnp.concatenate(parts, axis=0).T


def gate(place, mixed, q_own, q_far):
    ctx, halves, chans, cols = mixed.shape
    depth = ctx * halves * chans
    whole = lambda shape: pl.BlockSpec(shape, lambda i: (0,) * len(shape))
    return pl.pallas_call(
        gate_kernel,
        grid=(1,),
        in_specs=[pl.BlockSpec(memory_space=pltpu.SMEM), whole(mixed.shape), whole(q_own.shape), whole(q_far.shape)],
        out_specs=whole((cols, depth)),
        out_shape=jax.ShapeDtypeStruct((cols, depth), BF16),
        compiler_params=pltpu.CompilerParams(vmem_limit_bytes=VMEM_LIMIT),
        name="gate",
    )(place, mixed, q_own, q_far)


def project_kernel(last, place_ref, *refs):
    if last:
        g_ref, w_ref, sum_ref, out_ref = refs
    else:
        g_ref, w_ref, out_ref = refs
    halves, rows, block = w_ref.shape
    total = dot(g_ref[...], w_ref[...].reshape(halves * rows, block))
    if last:
        out_ref[...] = (total + sum_ref[...]).T.astype(BF16)
    else:
        out_ref[...] = total


def project(place, gated, weight, partial=None):
    depth, width = weight.shape
    cols = gated.shape[0]
    other = 0 if partial is None else 1
    block = 256
    in_specs = [
        pl.BlockSpec(gated.shape, lambda i, place: (0, 0)),
        pl.BlockSpec((2, None, depth // 4, block), lambda i, place: (0, jnp.bitwise_xor(place[3], other), 0, i)),
    ]
    operands = [gated, weight.reshape(2, 2, depth // 4, width)]
    if other:
        in_specs.append(pl.BlockSpec((cols, block), lambda i, place: (0, i)))
        operands.append(partial)
        out_spec = pl.BlockSpec((block, cols), lambda i, place: (i, 0))
        out_shape = jax.ShapeDtypeStruct((width, cols), BF16)
    else:
        out_spec = pl.BlockSpec((cols, block), lambda i, place: (0, i))
        out_shape = jax.ShapeDtypeStruct((cols, width), F32)
    return pl.pallas_call(
        lambda *refs: project_kernel(bool(other), *refs),
        grid_spec=pltpu.PrefetchScalarGridSpec(
            num_scalar_prefetch=1, grid=(width // block,), in_specs=in_specs, out_specs=out_spec
        ),
        out_shape=out_shape,
        compiler_params=pltpu.CompilerParams(vmem_limit_bytes=VMEM_LIMIT - 3 * 1024 * 1024),
        cost_estimate=pl.CostEstimate(flops=depth * width * cols, bytes_accessed=depth * width, transcendentals=0),
        name="project_last" if other else "project_first",
    )(place, *operands)


def turned(value, axis, steps):
    count = lax.axis_size(axis)
    return lax.ppermute(value, axis, [(source, (source + steps) % count) for source in range(count)])


def shards(query_proj, key_proj, value_proj, short_taps, long_filter, skip_bias, out_weight):
    rows, cols = query_proj.shape
    ctx = lax.axis_size(CTX)
    chans = long_filter.shape[0]
    tables = dft_tables(ctx, cols)

    taps = jnp.swapaxes(short_taps, 1, 2)
    place = jnp.stack([lax.axis_index(name) for name in (CTX, "zl", "zh", "core")]).astype(jnp.int32)

    pieces = [turned(out_weight, "zl", step) for step in (1, 2, 3)]
    ready = short_filters(taps, key_proj, value_proj, ctx)
    tail = take_tail(query_proj)
    rim = lax.ppermute(tail, CTX, [(source, source + 1) for source in range(ctx - 1)])
    ready, rim, *pieces = lax.optimization_barrier((ready, rim, *pieces))
    weight_run = jnp.concatenate([out_weight, *pieces], axis=0)
    weight = lax.all_gather(weight_run, ("y", "x"), axis=0, tiled=True)

    arrived = lax.all_to_all(ready, CTX, split_axis=0, concat_axis=0, tiled=True)
    q_feat = query_filter(taps, query_proj, rim)
    q_far = turned(q_feat, "zh", 1)
    long_filter, q_feat = lax.optimization_barrier((long_filter, q_feat))
    spectrum = filter_spectrum(long_filter, tables, ctx, cols)

    mixed = long_mix(place, arrived, spectrum, skip_bias, taps, tables, 2)
    mixed, q_far = lax.optimization_barrier((mixed, q_far))
    own = lax.all_to_all(
        mixed.reshape(2 * ctx, chans, cols), CTX + ("zh",), split_axis=0, concat_axis=0, tiled=True
    ).reshape(ctx, 2, chans, cols)
    gated = gate(place, own, q_feat, q_far)
    other = turned(gated, "core", 1)
    return project(place, other, weight, project(place, gated, weight))


def solution(mesh):
    fine = Mesh(mesh.devices.reshape(4, 4, 4, 2, 2), ("y", "x", "zl", "zh", "core"))
    mp = ("zh", "core")
    return jax.shard_map(
        shards,
        mesh=fine,
        in_specs=(
            P(mp, CTX),
            P(mp, CTX),
            P(mp, CTX),
            P(None, mp, None),
            P(mp + CTX, None),
            P(mp + CTX),
            P(CTX, mp),
        ),
        out_specs=P(mp, CTX),
        check_vma=False,
    )
```

```python
import math

import jax
import jax.numpy as jnp
import numpy as np
from jax import lax
from jax.experimental import pallas as pl
from jax.experimental.pallas import tpu as pltpu
from jax.sharding import Mesh, PartitionSpec as P

BF16 = jnp.bfloat16
F32 = jnp.float32
CTX = ("y", "x", "zl")
MIB = 1024 * 1024
VMEM_LIMIT = 60 * MIB


def hi_lo(table):
    hi = table.astype(np.float32).astype(jnp.bfloat16)
    lo = (table - hi.astype(np.float64)).astype(np.float32).astype(jnp.bfloat16)
    return hi, lo


def dft_tables(outer, inner):
    length = outer * inner
    freq = np.arange(outer)[:, None] + 0.25
    angle = 2.0 * np.pi * freq * np.arange(outer)[None, :] / outer
    first = np.concatenate([np.cos(angle), -np.sin(angle)], axis=0)
    spin = 2.0 * np.pi * freq * np.arange(inner)[None, :] / length
    steps = np.outer(np.arange(inner), np.arange(inner)) % inner
    turn = 2.0 * np.pi * steps / inner
    cos, sin = np.cos(turn), np.sin(turn)
    second = np.block([[cos, -sin], [sin, cos]])
    return {
        "first": hi_lo(first),
        "last": hi_lo(first.T.copy()),
        "spin": (np.cos(spin).astype(np.float32), np.sin(spin).astype(np.float32)),
        "second": hi_lo(second),
    }


def dot(left, right):
    return jnp.dot(left, right, preferred_element_type=F32)


def split_bf16(value):
    hi = value.astype(BF16)
    return hi, (value - hi.astype(F32)).astype(BF16)


def lane_ids(rows):
    return lax.broadcasted_iota(jnp.int32, (rows, 128), 1)


def filter_tiles(weights, before, tiles, lane):
    turned = {}
    for tap in range(1, len(weights)):
        for index, tile in enumerate(tiles):
            turned[index, tap] = pltpu.roll(tile, tap, 1)
        turned[-1, tap] = 0.0 if before is None else pltpu.roll(before, tap, 1)
    sums = []
    for index, tile in enumerate(tiles):
        total = weights[0] * tile
        for tap in range(1, len(weights)):
            total += weights[tap] * jnp.where(lane >= tap, turned[index, tap], turned[index - 1, tap])
        sums.append(total)
    return sums


def short_kernel(taps_ref, q_ref, k_ref, v_ref, out_ref):
    rows, cols = q_ref.shape
    taps = taps_ref.shape[1]
    size = out_ref.shape[1]
    first = pl.program_id(0) * (rows // size)
    lane = lane_ids(size)
    for g in range(rows // size):
        at = pl.ds(g * size, size)
        feats, edges = [], []
        for index, ref in ((1, k_ref), (2, v_ref)):
            wide = ref[at, :].astype(F32)
            tiles = [wide[:, i * 128 : i * 128 + 128] for i in range(cols // 128)]
            weights = [taps_ref[index, tap, first + g] for tap in range(taps)]
            feats.append(filter_tiles(weights, None, tiles, lane))
            shift = 8 if index == 1 else 24
            edges += [pltpu.roll(tiles[-1], shift, 1), pltpu.roll(tiles[0], shift, 1)]
        for i in range(cols // 128):
            out_ref[g, :, i * 128 : i * 128 + 128] = (feats[0][i] * feats[1][i]).astype(BF16)
        out_ref[g, :, cols : 2 * cols] = q_ref[at, :]
        edge = jnp.where(lane < 16, jnp.where(lane < 8, edges[0], edges[1]), jnp.where(lane < 24, edges[2], edges[3]))
        out_ref[g, :, 2 * cols :] = edge.astype(BF16)


def short_filters(taps, query, key, value, ctx, blocks=4):
    rows, cols = query.shape
    size = rows // ctx
    spec = pl.BlockSpec((rows // blocks, cols), lambda i: (i, 0))
    return pl.pallas_call(
        short_kernel,
        grid=(blocks,),
        in_specs=[pl.BlockSpec(memory_space=pltpu.SMEM)] + [spec] * 3,
        out_specs=pl.BlockSpec((ctx // blocks, size, 2 * cols + 128), lambda i: (i, 0, 0)),
        out_shape=jax.ShapeDtypeStruct((ctx, size, 2 * cols + 128), BF16),
        compiler_params=pltpu.CompilerParams(vmem_limit_bytes=VMEM_LIMIT),
        cost_estimate=pl.CostEstimate(flops=2 * 14 * rows * cols, bytes_accessed=10 * rows * cols, transcendentals=0),
        name="short_filters",
    )(taps, query, key, value)


def second_dft(hi, lo, second_hi, second_lo):
    return dot(hi, second_hi[...]) + dot(lo, second_hi[...]) + dot(hi, second_lo[...])


def channel_rows(ref, c, outer, chans):
    halves = ref.shape[0] // (outer * chans)
    parts = [ref[pl.ds(half * outer * chans + c, outer, stride=chans), :] for half in range(halves)]
    return jnp.concatenate(parts, axis=1)


def filter_kernel(scale, filt_ref, f_hi, f_lo, cos_ref, sin_ref, s_hi, s_lo, out_ref, rows_ref, g_hi, g_lo):
    chans, _ = filt_ref.shape
    outer, inner = cos_ref.shape
    for half in range(inner // 128):
        for a in range(outer):
            start = a * inner + half * 128
            at = (half * outer + a) * chans
            rows_ref[at : at + chans, :] = filt_ref[:, start : start + 128]

    for c in range(chans):
        hi, lo = split_bf16(channel_rows(rows_ref, c, outer, chans) * scale)
        mixed = dot(f_hi[...], hi) + dot(f_hi[...], lo) + dot(f_lo[...], hi)
        re, im = mixed[:outer], mixed[outer:]
        at = pl.ds(c * outer, outer)
        g_hi[at, :inner], g_lo[at, :inner] = split_bf16(re * cos_ref[...] + im * sin_ref[...])
        g_hi[at, inner:], g_lo[at, inner:] = split_bf16(im * cos_ref[...] - re * sin_ref[...])

    for i in range(chans * outer // 256):
        at = pl.ds(i * 256, 256)
        out_ref[at, :] = second_dft(g_hi[at, :], g_lo[at, :], s_hi, s_lo)


def filter_spectrum(long_filter, tables, outer, inner):
    chans = long_filter.shape[0]
    rows = chans * outer
    whole = lambda shape: pl.BlockSpec(shape, lambda i: (0,) * len(shape))
    operands = (long_filter, *tables["first"], *tables["spin"], *tables["second"])
    return pl.pallas_call(
        lambda *refs: filter_kernel(1.0 / (outer * inner), *refs),
        grid=(1,),
        in_specs=[whole(operand.shape) for operand in operands],
        out_specs=whole((rows, 2 * inner)),
        out_shape=jax.ShapeDtypeStruct((rows, 2 * inner), F32),
        scratch_shapes=[
            pltpu.VMEM((rows * inner // 128, 128), F32),
            pltpu.VMEM((rows, 2 * inner), BF16),
            pltpu.VMEM((rows, 2 * inner), BF16),
        ],
        compiler_params=pltpu.CompilerParams(vmem_limit_bytes=VMEM_LIMIT),
        cost_estimate=pl.CostEstimate(flops=3 * 2 * rows * 4 * inner * inner, bytes_accessed=5 * 2**20, transcendentals=0),
        name="filter_spectrum",
    )(*operands)


def conv_kernel(
    place_ref, skip_ref, taps_ref, in_ref, f_hi, f_lo, l_hi, l_lo, cos_ref, sin_ref, spec_hbm, s_hi_hbm, s_lo_hbm,
    out_ref, rows_ref, z_ref, q_ref, edge_ref, g_hi, g_lo, spec_ref, s_hi, s_lo, sems,
):
    fetches = [
        pltpu.make_async_copy(source, target, sems.at[index])
        for index, (source, target) in enumerate(((spec_hbm, spec_ref), (s_hi_hbm, s_hi), (s_lo_hbm, s_lo)))
    ]
    for fetch in fetches:
        fetch.start()
    outer, chans, width = in_ref.shape
    inner = (width - 128) // 2
    halves = inner // 128
    rows = outer * chans
    taps = taps_ref.shape[1]
    group = place_ref[0]
    blocks = 8
    step = rows // blocks
    units = outer // blocks
    lane = lane_ids(step)

    edge_ref[:chans, :] = jnp.zeros((chans, 128), F32)
    q_ref[(halves - 1) * (rows + chans) : (halves - 1) * (rows + chans) + chans, :] = jnp.zeros((chans, 128), F32)
    edge_ref[chans:, :] = in_ref[:, :, 2 * inner :].reshape(rows, 128).astype(F32)
    for half in range(halves):
        at = half * (rows + chans) + chans
        q_ref[at : at + rows, :] = (
            in_ref[:, :, inner + half * 128 : inner + half * 128 + 128].reshape(rows, 128).astype(F32)
        )

    weights = [jnp.where(lane < 16, taps_ref[1, tap, group], taps_ref[2, tap, group]) for tap in range(taps)]

    for i in range(blocks):
        at = i * step
        edge = jnp.where(jnp.bitwise_and(lane, 8) == 0, edge_ref[at : at + step, :], edge_ref[at + chans : at + chans + step, :])
        total = weights[0] * edge
        for tap in range(1, taps):
            total += weights[tap] * pltpu.roll(edge, tap, 1)
        first = (pltpu.roll(total, 120, 1) * pltpu.roll(total, 104, 1)).astype(BF16).astype(F32)
        sig = in_ref[i * units : (i + 1) * units, :, :inner].reshape(step, inner).astype(F32)
        rows_ref[at : at + step, :] = jnp.where(lane < taps - 1, first, sig[:, :128])
        for half in range(1, halves):
            rows_ref[half * rows + at : half * rows + at + step, :] = sig[:, half * 128 : half * 128 + 128]

    for c in range(chans):
        sig = channel_rows(rows_ref, c, outer, chans).astype(BF16)
        mixed = dot(f_hi[...], sig) + dot(f_lo[...], sig)
        re, im = mixed[:outer], mixed[outer:]
        at = pl.ds(c * outer, outer)
        g_hi[at, :inner], g_lo[at, :inner] = split_bf16(re * cos_ref[...] + im * sin_ref[...])
        g_hi[at, inner:], g_lo[at, inner:] = split_bf16(im * cos_ref[...] - re * sin_ref[...])

    for fetch in fetches:
        fetch.wait()

    block = min(chans * outer, 512)
    for i in range(chans * outer // block):
        at = pl.ds(i * block, block)
        sig = second_dft(g_hi[at, :], g_lo[at, :], s_hi, s_lo)
        sr, si = sig[:, :inner], sig[:, inner:]
        hr, hm = spec_ref[at, :inner], spec_ref[at, inner:]
        r_hi, r_lo = split_bf16(sr * hr - si * hm)
        i_hi, i_lo = split_bf16(-(sr * hm + si * hr))
        back = second_dft(
            jnp.concatenate([r_hi, i_hi], axis=1), jnp.concatenate([r_lo, i_lo], axis=1), s_hi, s_lo
        )
        back = back.reshape(block // outer, outer, 2 * inner)
        re, im = back[:, :, :inner], back[:, :, inner:]
        cos, sin = cos_ref[...], sin_ref[...]
        r_hi, r_lo = split_bf16((re * cos + im * sin).reshape(block, inner))
        i_hi, i_lo = split_bf16((re * sin - im * cos).reshape(block, inner))
        for j in range(block // outer):
            c = i * (block // outer) + j
            part = slice(j * outer, (j + 1) * outer)
            hi = jnp.concatenate([r_hi[part], i_hi[part]], axis=0)
            lo = jnp.concatenate([r_lo[part], i_lo[part]], axis=0)
            conv = dot(l_hi[...], hi) + dot(l_hi[...], lo) + dot(l_lo[...], hi)
            mixed = conv + skip_ref[c] * channel_rows(rows_ref, c, outer, chans)
            for half in range(halves):
                z_ref[pl.ds(half * rows + c, outer, stride=chans), :] = mixed[:, half * 128 : (half + 1) * 128]

    q_taps = [taps_ref[0, tap, group] for tap in range(taps)]
    for i in range(blocks):
        at = i * step
        starts = [half * (rows + chans) + chans + at for half in range(halves)]
        tiles = [q_ref[start : start + step, :] for start in starts]
        start = (halves - 1) * (rows + chans) + at
        feats = filter_tiles(q_taps, q_ref[start : start + step, :], tiles, lane)
        for half in range(halves):
            mixed = z_ref[half * rows + at : half * rows + at + step, :].astype(BF16).astype(F32)
            result = (feats[half] * mixed).astype(BF16).reshape(units, chans, 128)
            for copy in range(out_ref.shape[1]):
                out_ref[i * units : (i + 1) * units, copy, :, half * 128 : (half + 1) * 128] = result


def long_mix(place, arrived, spectrum, skip_bias, taps, tables, copies):
    outer, chans, width = arrived.shape
    inner = (width - 128) // 2
    rows = outer * chans
    whole = lambda shape: pl.BlockSpec(shape, lambda i: (0,) * len(shape))
    scalars = pl.BlockSpec(memory_space=pltpu.SMEM)
    operands = (arrived, *tables["first"], *tables["last"], *tables["spin"])
    fetched = (spectrum, *tables["second"])
    return pl.pallas_call(
        conv_kernel,
        grid=(1,),
        in_specs=[scalars] * 3
        + [whole(operand.shape) for operand in operands]
        + [pl.BlockSpec(memory_space=pl.ANY)] * len(fetched),
        out_specs=whole((outer, copies, chans, inner)),
        out_shape=jax.ShapeDtypeStruct((outer, copies, chans, inner), BF16),
        scratch_shapes=[
            pltpu.VMEM((rows * inner // 128, 128), F32),
            pltpu.VMEM((rows * inner // 128, 128), F32),
            pltpu.VMEM(((rows + chans) * inner // 128, 128), F32),
            pltpu.VMEM((rows + chans, 128), F32),
            pltpu.VMEM((rows, 2 * inner), BF16),
            pltpu.VMEM((rows, 2 * inner), BF16),
            pltpu.VMEM((rows, 2 * inner), F32),
            pltpu.VMEM((2 * inner, 2 * inner), BF16),
            pltpu.VMEM((2 * inner, 2 * inner), BF16),
            pltpu.SemaphoreType.DMA((3,)),
        ],
        compiler_params=pltpu.CompilerParams(vmem_limit_bytes=VMEM_LIMIT),
        cost_estimate=pl.CostEstimate(flops=2**20, bytes_accessed=2**20, transcendentals=0),
        name="long_conv",
    )(place, skip_bias, taps, *operands, *fetched)


def project_kernel(other, place_ref, z_hbm, *refs):
    extras, refs = refs[:4], refs[4:]
    if other:
        w_hbm, sum_hbm, out_hbm, z_ref, w_ref, g_ref, out_ref, sum_ref, sems = refs
    else:
        w_hbm, out_hbm, z_ref, w_ref, g_ref, out_ref, sems = refs
    _, halves, chans, cols = z_ref.shape
    depth, width = w_ref.shape
    unit = 4 * chans
    size = 4 * unit
    run = size - unit
    block = 256
    y, x_here, zl = place_ref[4], place_ref[5], place_ref[1]
    core = jnp.bitwise_xor(place_ref[3], other)

    def copy(source, target, index):
        fetch = pltpu.make_async_copy(source, target, sems.at[index])
        fetch.start()
        return fetch

    arriving = copy(z_hbm, z_ref, 0)
    fetches = []
    for half in range(halves):
        for x in range(4):
            index = half * 4 + x
            at = index * size
            panel = half * 2 + core
            start = pl.multiple_of((panel * 4 + x) * run, unit)
            fetches.append(copy(w_hbm.at[pl.ds(start, run)], w_ref.at[pl.ds(at, run)], 1 + index))
            start = pl.multiple_of(jnp.bitwise_and(x_here - x, 3) * unit, unit)
            for turn, extra in enumerate(extras):

                @pl.when(jnp.bitwise_and(y - panel, 3) == turn)
                def _():
                    copy(extra.at[pl.ds(start, unit)], w_ref.at[pl.ds(at + run, unit)], 9 + index)

            fetches.append(
                pltpu.make_async_copy(extras[0].at[pl.ds(start, unit)], w_ref.at[pl.ds(at + run, unit)], sems.at[9 + index])
            )
    if other:
        fetches.append(copy(sum_hbm, sum_ref, 17))
    arriving.wait()
    for half in range(halves):
        for x in range(4):
            parts = []
            for turn in range(4):
                start = x * 16 + 4 * jnp.bitwise_and(zl - turn, 3)
                parts.append(z_ref[pl.ds(start, 4), half].reshape(unit, cols))
            to = (half * 4 + x) * size
            g_ref[:, to : to + size] = jnp.concatenate(parts, axis=0).T
    for fetch in fetches:
        fetch.wait()
    leaving = []
    for index in range(width // block):
        at = slice(index * block, (index + 1) * block)
        part = dot(g_ref[...], w_ref[:, at])
        if other:
            out_ref[at, :] = (part + sum_ref[:, at]).T.astype(BF16)
            leaving.append(copy(out_ref.at[at], out_hbm.at[at], 18 + index))
        else:
            out_ref[index] = part
            leaving.append(copy(out_ref.at[index], out_hbm.at[:, at], 18 + index))
    for leave in leaving:
        leave.wait()


def project(place, gated, weight, extras, partial=None):
    width = weight.shape[1]
    depth = (weight.shape[0] + 4 * extras[0].shape[0]) // 2
    cols = gated.shape[3]
    other = 0 if partial is None else 1
    anywhere = pl.BlockSpec(memory_space=pl.ANY)
    operands = [gated, *extras, weight] + ([partial] if other else [])
    shape = (width, cols) if other else (cols, width)
    return pl.pallas_call(
        lambda *refs: project_kernel(other, *refs),
        in_specs=[pl.BlockSpec(memory_space=pltpu.SMEM)] + [anywhere] * len(operands),
        out_specs=anywhere,
        out_shape=jax.ShapeDtypeStruct(shape, BF16 if other else F32),
        scratch_shapes=[
            pltpu.VMEM(gated.shape, BF16),
            pltpu.VMEM((depth, width), BF16),
            pltpu.VMEM((cols, depth), BF16),
            pltpu.VMEM(shape, BF16) if other else pltpu.VMEM((width // 256, cols, 256), F32),
        ]
        + ([pltpu.VMEM((cols, width), F32)] if other else [])
        + [pltpu.SemaphoreType.DMA((18 + width // 256,))],
        compiler_params=pltpu.CompilerParams(vmem_limit_bytes=VMEM_LIMIT),
        cost_estimate=pl.CostEstimate(flops=2 * depth * width * cols, bytes_accessed=2 * depth * width, transcendentals=0),
        name="project_last" if other else "project_first",
    )(place, *operands)


def turned(value, axis, steps):
    count = lax.axis_size(axis)
    return lax.ppermute(value, axis, [(source, (source + steps) % count) for source in range(count)])


def shards(query_proj, key_proj, value_proj, short_taps, long_filter, skip_bias, out_weight):
    rows, cols = query_proj.shape
    ctx = lax.axis_size(CTX)
    chans = long_filter.shape[0]
    tables = dft_tables(ctx, cols)

    taps = jnp.swapaxes(short_taps, 1, 2)
    place = jnp.stack([lax.axis_index(name) for name in (CTX, "zl", "zh", "core", "y", "x")]).astype(jnp.int32)

    pieces = [turned(out_weight, "zl", step) for step in (1, 2, 3)]
    ready = short_filters(taps, query_proj, key_proj, value_proj, ctx)
    ready, *pieces = lax.optimization_barrier((ready, *pieces))
    weight = lax.all_gather(jnp.concatenate([out_weight, *pieces[:2]], axis=0), ("y", "x"), axis=0, tiled=True)

    spectrum = filter_spectrum(long_filter, tables, ctx, cols)
    arrived = lax.all_to_all(ready, CTX, split_axis=0, concat_axis=0, tiled=True)

    spectrum, last_piece = lax.optimization_barrier((spectrum, pieces[2]))
    along_x = jnp.concatenate([last_piece] + [turned(last_piece, "x", step) for step in (1, 2, 3)], axis=0)
    along_y = [turned(along_x, "y", step) for step in (1, 2, 3)]

    gated = long_mix(place, arrived, spectrum, skip_bias, taps, tables, 2)
    gated, *along_y = lax.optimization_barrier((gated, *along_y))
    extras = [along_x, *along_y]
    own = lax.all_to_all(
        gated.reshape(2 * ctx, chans, cols), CTX + ("zh",), split_axis=0, concat_axis=0, tiled=True
    ).reshape(ctx, 2, chans, cols)
    other = turned(own, "core", 1)
    return project(place, other, weight, extras, project(place, own, weight, extras))


def solution(mesh):
    fine = Mesh(mesh.devices.reshape(4, 4, 4, 2, 2), ("y", "x", "zl", "zh", "core"))
    mp = ("zh", "core")
    return jax.shard_map(
        shards,
        mesh=fine,
        in_specs=(
            P(mp, CTX),
            P(mp, CTX),
            P(mp, CTX),
            P(None, mp, None),
            P(mp + CTX, None),
            P(mp + CTX),
            P(CTX, mp),
        ),
        out_specs=P(mp, CTX),
        check_vma=False,
    )
```

```python
import math

import jax
import jax.numpy as jnp
import numpy as np
from jax import lax
from jax.experimental import pallas as pl
from jax.experimental.pallas import tpu as pltpu
from jax.sharding import Mesh, PartitionSpec as P

BF16 = jnp.bfloat16
F32 = jnp.float32
CTX = ("y", "x", "zl")
MIB = 1024 * 1024
VMEM_LIMIT = 60 * MIB


def hi_lo(table):
    hi = table.astype(np.float32).astype(jnp.bfloat16)
    lo = (table - hi.astype(np.float64)).astype(np.float32).astype(jnp.bfloat16)
    return hi, lo


def dft_tables(outer, inner):
    length = outer * inner
    freq = np.arange(outer)[:, None] + 0.25
    angle = 2.0 * np.pi * freq * np.arange(outer)[None, :] / outer
    first = np.concatenate([np.cos(angle), -np.sin(angle)], axis=0)
    spin = 2.0 * np.pi * freq * np.arange(inner)[None, :] / length
    steps = np.outer(np.arange(inner), np.arange(inner)) % inner
    turn = 2.0 * np.pi * steps / inner
    cos, sin = np.cos(turn), np.sin(turn)
    second = np.block([[cos, -sin], [sin, cos]])
    return {
        "first": hi_lo(first),
        "last": hi_lo(first.T.copy()),
        "spin": (np.cos(spin).astype(np.float32), np.sin(spin).astype(np.float32)),
        "second": hi_lo(second),
    }


def dot(left, right):
    return jnp.dot(left, right, preferred_element_type=F32)


def split_bf16(value):
    hi = value.astype(BF16)
    return hi, (value - hi.astype(F32)).astype(BF16)


def lane_ids(rows):
    return lax.broadcasted_iota(jnp.int32, (rows, 128), 1)


def filter_tiles(weights, before, tiles, lane):
    turned = {}
    for tap in range(1, len(weights)):
        for index, tile in enumerate(tiles):
            turned[index, tap] = pltpu.roll(tile, tap, 1)
        turned[-1, tap] = 0.0 if before is None else pltpu.roll(before, tap, 1)
    sums = []
    for index, tile in enumerate(tiles):
        total = weights[0] * tile
        for tap in range(1, len(weights)):
            total += weights[tap] * jnp.where(lane >= tap, turned[index, tap], turned[index - 1, tap])
        sums.append(total)
    return sums


def short_kernel(taps_ref, q_ref, k_ref, v_ref, out_ref):
    rows, cols = q_ref.shape
    taps = taps_ref.shape[1]
    size = out_ref.shape[1]
    first = pl.program_id(0) * (rows // size)
    lane = lane_ids(size)
    for g in range(rows // size):
        at = pl.ds(g * size, size)
        feats, edges = [], []
        for index, ref in ((1, k_ref), (2, v_ref)):
            wide = ref[at, :].astype(F32)
            tiles = [wide[:, i * 128 : i * 128 + 128] for i in range(cols // 128)]
            weights = [taps_ref[index, tap, first + g] for tap in range(taps)]
            feats.append(filter_tiles(weights, None, tiles, lane))
            shift = 8 if index == 1 else 24
            edges += [pltpu.roll(tiles[-1], shift, 1), pltpu.roll(tiles[0], shift, 1)]
        for i in range(cols // 128):
            out_ref[g, :, i * 128 : i * 128 + 128] = (feats[0][i] * feats[1][i]).astype(BF16)
        out_ref[g, :, cols : 2 * cols] = q_ref[at, :]
        edge = jnp.where(lane < 16, jnp.where(lane < 8, edges[0], edges[1]), jnp.where(lane < 24, edges[2], edges[3]))
        out_ref[g, :, 2 * cols :] = edge.astype(BF16)


def short_filters(taps, query, key, value, ctx, blocks=4):
    rows, cols = query.shape
    size = rows // ctx
    spec = pl.BlockSpec((rows // blocks, cols), lambda i: (i, 0))
    return pl.pallas_call(
        short_kernel,
        grid=(blocks,),
        in_specs=[pl.BlockSpec(memory_space=pltpu.SMEM)] + [spec] * 3,
        out_specs=pl.BlockSpec((ctx // blocks, size, 2 * cols + 128), lambda i: (i, 0, 0)),
        out_shape=jax.ShapeDtypeStruct((ctx, size, 2 * cols + 128), BF16),
        compiler_params=pltpu.CompilerParams(vmem_limit_bytes=VMEM_LIMIT),
        cost_estimate=pl.CostEstimate(flops=2 * 14 * rows * cols, bytes_accessed=10 * rows * cols, transcendentals=0),
        name="short_filters",
    )(taps, query, key, value)


def second_dft(hi, lo, second_hi, second_lo):
    return dot(hi, second_hi[...]) + dot(lo, second_hi[...]) + dot(hi, second_lo[...])


def channel_rows(ref, c, outer, chans):
    halves = ref.shape[0] // (outer * chans)
    parts = [ref[pl.ds(half * outer * chans + c, outer, stride=chans), :] for half in range(halves)]
    return jnp.concatenate(parts, axis=1)


def filter_kernel(scale, filt_ref, f_hi, f_lo, cos_ref, sin_ref, s_hi, s_lo, out_ref, rows_ref, g_hi, g_lo):
    chans, _ = filt_ref.shape
    outer, inner = cos_ref.shape
    for half in range(inner // 128):
        for a in range(outer):
            start = a * inner + half * 128
            at = (half * outer + a) * chans
            rows_ref[at : at + chans, :] = filt_ref[:, start : start + 128]

    for c in range(chans):
        hi, lo = split_bf16(channel_rows(rows_ref, c, outer, chans) * scale)
        mixed = dot(f_hi[...], hi) + dot(f_hi[...], lo) + dot(f_lo[...], hi)
        re, im = mixed[:outer], mixed[outer:]
        at = pl.ds(c * outer, outer)
        g_hi[at, :inner], g_lo[at, :inner] = split_bf16(re * cos_ref[...] + im * sin_ref[...])
        g_hi[at, inner:], g_lo[at, inner:] = split_bf16(im * cos_ref[...] - re * sin_ref[...])

    for i in range(chans * outer // 256):
        at = pl.ds(i * 256, 256)
        out_ref[at, :] = second_dft(g_hi[at, :], g_lo[at, :], s_hi, s_lo)


def filter_spectrum(long_filter, tables, outer, inner):
    chans = long_filter.shape[0]
    rows = chans * outer
    whole = lambda shape: pl.BlockSpec(shape, lambda i: (0,) * len(shape))
    operands = (long_filter, *tables["first"], *tables["spin"], *tables["second"])
    return pl.pallas_call(
        lambda *refs: filter_kernel(1.0 / (outer * inner), *refs),
        grid=(1,),
        in_specs=[whole(operand.shape) for operand in operands],
        out_specs=whole((rows, 2 * inner)),
        out_shape=jax.ShapeDtypeStruct((rows, 2 * inner), F32),
        scratch_shapes=[
            pltpu.VMEM((rows * inner // 128, 128), F32),
            pltpu.VMEM((rows, 2 * inner), BF16),
            pltpu.VMEM((rows, 2 * inner), BF16),
        ],
        compiler_params=pltpu.CompilerParams(vmem_limit_bytes=VMEM_LIMIT),
        cost_estimate=pl.CostEstimate(flops=3 * 2 * rows * 4 * inner * inner, bytes_accessed=5 * 2**20, transcendentals=0),
        name="filter_spectrum",
    )(*operands)


def conv_kernel(
    place_ref, skip_ref, taps_ref, in_ref, f_hi, f_lo, l_hi, l_lo, cos_ref, sin_ref, spec_hbm, s_hi_hbm, s_lo_hbm,
    out_ref, rows_ref, z_ref, q_ref, edge_ref, g_hi, g_lo, spec_ref, s_hi, s_lo, sems,
):
    fetches = [
        pltpu.make_async_copy(source, target, sems.at[index])
        for index, (source, target) in enumerate(((spec_hbm, spec_ref), (s_hi_hbm, s_hi), (s_lo_hbm, s_lo)))
    ]
    for fetch in fetches:
        fetch.start()
    outer, chans, width = in_ref.shape
    inner = (width - 128) // 2
    halves = inner // 128
    rows = outer * chans
    taps = taps_ref.shape[1]
    group = place_ref[0]
    blocks = 8
    step = rows // blocks
    units = outer // blocks
    lane = lane_ids(step)

    edge_ref[:chans, :] = jnp.zeros((chans, 128), F32)
    q_ref[(halves - 1) * (rows + chans) : (halves - 1) * (rows + chans) + chans, :] = jnp.zeros((chans, 128), F32)
    edge_ref[chans:, :] = in_ref[:, :, 2 * inner :].reshape(rows, 128).astype(F32)
    for half in range(halves):
        at = half * (rows + chans) + chans
        q_ref[at : at + rows, :] = (
            in_ref[:, :, inner + half * 128 : inner + half * 128 + 128].reshape(rows, 128).astype(F32)
        )

    weights = [jnp.where(lane < 16, taps_ref[1, tap, group], taps_ref[2, tap, group]) for tap in range(taps)]

    for i in range(blocks):
        at = i * step
        edge = jnp.where(jnp.bitwise_and(lane, 8) == 0, edge_ref[at : at + step, :], edge_ref[at + chans : at + chans + step, :])
        total = weights[0] * edge
        for tap in range(1, taps):
            total += weights[tap] * pltpu.roll(edge, tap, 1)
        first = (pltpu.roll(total, 120, 1) * pltpu.roll(total, 104, 1)).astype(BF16).astype(F32)
        sig = in_ref[i * units : (i + 1) * units, :, :inner].reshape(step, inner).astype(F32)
        rows_ref[at : at + step, :] = jnp.where(lane < taps - 1, first, sig[:, :128])
        for half in range(1, halves):
            rows_ref[half * rows + at : half * rows + at + step, :] = sig[:, half * 128 : half * 128 + 128]

    for c in range(chans):
        sig = channel_rows(rows_ref, c, outer, chans).astype(BF16)
        mixed = dot(f_hi[...], sig) + dot(f_lo[...], sig)
        re, im = mixed[:outer], mixed[outer:]
        at = pl.ds(c * outer, outer)
        g_hi[at, :inner], g_lo[at, :inner] = split_bf16(re * cos_ref[...] + im * sin_ref[...])
        g_hi[at, inner:], g_lo[at, inner:] = split_bf16(im * cos_ref[...] - re * sin_ref[...])

    for fetch in fetches:
        fetch.wait()

    block = min(chans * outer, 512)
    for i in range(chans * outer // block):
        at = pl.ds(i * block, block)
        sig = second_dft(g_hi[at, :], g_lo[at, :], s_hi, s_lo)
        sr, si = sig[:, :inner], sig[:, inner:]
        hr, hm = spec_ref[at, :inner], spec_ref[at, inner:]
        r_hi, r_lo = split_bf16(sr * hr - si * hm)
        i_hi, i_lo = split_bf16(-(sr * hm + si * hr))
        back = second_dft(
            jnp.concatenate([r_hi, i_hi], axis=1), jnp.concatenate([r_lo, i_lo], axis=1), s_hi, s_lo
        )
        back = back.reshape(block // outer, outer, 2 * inner)
        re, im = back[:, :, :inner], back[:, :, inner:]
        cos, sin = cos_ref[...], sin_ref[...]
        r_hi, r_lo = split_bf16((re * cos + im * sin).reshape(block, inner))
        i_hi, i_lo = split_bf16((re * sin - im * cos).reshape(block, inner))
        for j in range(block // outer):
            c = i * (block // outer) + j
            part = slice(j * outer, (j + 1) * outer)
            hi = jnp.concatenate([r_hi[part], i_hi[part]], axis=0)
            lo = jnp.concatenate([r_lo[part], i_lo[part]], axis=0)
            conv = dot(l_hi[...], hi) + dot(l_hi[...], lo) + dot(l_lo[...], hi)
            mixed = conv + skip_ref[c] * channel_rows(rows_ref, c, outer, chans)
            for half in range(halves):
                z_ref[pl.ds(half * rows + c, outer, stride=chans), :] = mixed[:, half * 128 : (half + 1) * 128]

    q_taps = [taps_ref[0, tap, group] for tap in range(taps)]
    for i in range(blocks):
        at = i * step
        starts = [half * (rows + chans) + chans + at for half in range(halves)]
        tiles = [q_ref[start : start + step, :] for start in starts]
        start = (halves - 1) * (rows + chans) + at
        feats = filter_tiles(q_taps, q_ref[start : start + step, :], tiles, lane)
        for half in range(halves):
            mixed = z_ref[half * rows + at : half * rows + at + step, :].astype(BF16).astype(F32)
            result = (feats[half] * mixed).astype(BF16).reshape(units, chans, 128)
            for copy in range(out_ref.shape[1]):
                out_ref[i * units : (i + 1) * units, copy, :, half * 128 : (half + 1) * 128] = result


def long_mix(place, arrived, spectrum, skip_bias, taps, tables, copies):
    outer, chans, width = arrived.shape
    inner = (width - 128) // 2
    rows = outer * chans
    whole = lambda shape: pl.BlockSpec(shape, lambda i: (0,) * len(shape))
    scalars = pl.BlockSpec(memory_space=pltpu.SMEM)
    operands = (arrived, *tables["first"], *tables["last"], *tables["spin"])
    fetched = (spectrum, *tables["second"])
    return pl.pallas_call(
        conv_kernel,
        grid=(1,),
        in_specs=[scalars] * 3
        + [whole(operand.shape) for operand in operands]
        + [pl.BlockSpec(memory_space=pl.ANY)] * len(fetched),
        out_specs=whole((outer, copies, chans, inner)),
        out_shape=jax.ShapeDtypeStruct((outer, copies, chans, inner), BF16),
        scratch_shapes=[
            pltpu.VMEM((rows * inner // 128, 128), F32),
            pltpu.VMEM((rows * inner // 128, 128), F32),
            pltpu.VMEM(((rows + chans) * inner // 128, 128), F32),
            pltpu.VMEM((rows + chans, 128), F32),
            pltpu.VMEM((rows, 2 * inner), BF16),
            pltpu.VMEM((rows, 2 * inner), BF16),
            pltpu.VMEM((rows, 2 * inner), F32),
            pltpu.VMEM((2 * inner, 2 * inner), BF16),
            pltpu.VMEM((2 * inner, 2 * inner), BF16),
            pltpu.SemaphoreType.DMA((3,)),
        ],
        compiler_params=pltpu.CompilerParams(vmem_limit_bytes=VMEM_LIMIT - 12 * MIB),
        cost_estimate=pl.CostEstimate(flops=2**20, bytes_accessed=2**20, transcendentals=0),
        name="long_conv",
    )(place, skip_bias, taps, *operands, *fetched)


def project_kernel(other, place_ref, z_hbm, *refs):
    if other:
        w_hbm, sum_hbm, out_hbm, z_ref, w_ref, g_ref, out_ref, sum_ref, sems = refs
    else:
        w_hbm, out_hbm, z_ref, w_ref, g_ref, out_ref, sems = refs
    _, halves, chans, cols = z_ref.shape
    depth, width = w_ref.shape
    unit = 4 * chans
    size = 4 * unit
    block = 256
    zl = place_ref[1]
    core = jnp.bitwise_xor(place_ref[3], other)

    def copy(source, target, index):
        fetch = pltpu.make_async_copy(source, target, sems.at[index])
        fetch.start()
        return fetch

    arriving = copy(z_hbm, z_ref, 0)
    fetches = []
    for half in range(halves):
        for x in range(4):
            index = half * 4 + x
            start = pl.multiple_of(((half * 2 + core) * 4 + x) * size, size)
            fetches.append(copy(w_hbm.at[pl.ds(start, size)], w_ref.at[pl.ds(index * size, size)], 1 + index))
    if other:
        fetches.append(copy(sum_hbm, sum_ref, 9))
    arriving.wait()
    for half in range(halves):
        for x in range(4):
            parts = []
            for turn in range(4):
                start = x * 16 + 4 * jnp.bitwise_and(zl - turn, 3)
                parts.append(z_ref[pl.ds(start, 4), half].reshape(unit, cols))
            to = (half * 4 + x) * size
            g_ref[:, to : to + size] = jnp.concatenate(parts, axis=0).T
    for fetch in fetches:
        fetch.wait()
    leaving = []
    for index in range(width // block):
        at = slice(index * block, (index + 1) * block)
        part = dot(g_ref[...], w_ref[:, at])
        if other:
            out_ref[at, :] = (part + sum_ref[:, at]).T.astype(BF16)
            leaving.append(copy(out_ref.at[at], out_hbm.at[at], 10 + index))
        else:
            out_ref[index] = part
            leaving.append(copy(out_ref.at[index], out_hbm.at[:, at], 10 + index))
    for leave in leaving:
        leave.wait()


def project(place, gated, weight, partial=None):
    width = weight.shape[1]
    depth = weight.shape[0] // 2
    cols = gated.shape[3]
    other = 0 if partial is None else 1
    anywhere = pl.BlockSpec(memory_space=pl.ANY)
    operands = [gated, weight] + ([partial] if other else [])
    shape = (width, cols) if other else (cols, width)
    return pl.pallas_call(
        lambda *refs: project_kernel(other, *refs),
        in_specs=[pl.BlockSpec(memory_space=pltpu.SMEM)] + [anywhere] * len(operands),
        out_specs=anywhere,
        out_shape=jax.ShapeDtypeStruct(shape, BF16 if other else F32),
        scratch_shapes=[
            pltpu.VMEM(gated.shape, BF16),
            pltpu.VMEM((depth, width), BF16),
            pltpu.VMEM((cols, depth), BF16),
            pltpu.VMEM(shape, BF16) if other else pltpu.VMEM((width // 256, cols, 256), F32),
        ]
        + ([pltpu.VMEM((cols, width), F32)] if other else [])
        + [pltpu.SemaphoreType.DMA((10 + width // 256,))],
        compiler_params=pltpu.CompilerParams(vmem_limit_bytes=VMEM_LIMIT - 12 * MIB),
        cost_estimate=pl.CostEstimate(flops=2 * depth * width * cols, bytes_accessed=2 * depth * width, transcendentals=0),
        name="project_last" if other else "project_first",
    )(place, *operands)


def turned(value, axis, steps):
    count = lax.axis_size(axis)
    return lax.ppermute(value, axis, [(source, (source + steps) % count) for source in range(count)])


def shards(query_proj, key_proj, value_proj, short_taps, long_filter, skip_bias, out_weight):
    rows, cols = query_proj.shape
    ctx = lax.axis_size(CTX)
    chans = long_filter.shape[0]
    tables = dft_tables(ctx, cols)

    taps = jnp.swapaxes(short_taps, 1, 2)
    place = jnp.stack([lax.axis_index(name) for name in (CTX, "zl", "zh", "core")]).astype(jnp.int32)

    pieces = [turned(out_weight, "zl", step) for step in (1, 2, 3)]
    ready = short_filters(taps, query_proj, key_proj, value_proj, ctx)
    ready, *pieces = lax.optimization_barrier((ready, *pieces))
    weight = lax.all_gather(jnp.concatenate([out_weight, *pieces], axis=0), ("y", "x"), axis=0, tiled=True)

    spectrum = filter_spectrum(long_filter, tables, ctx, cols)
    arrived = lax.all_to_all(ready, CTX, split_axis=0, concat_axis=0, tiled=True)
    gated = long_mix(place, arrived, spectrum, skip_bias, taps, tables, 2)
    own = lax.all_to_all(
        gated.reshape(2 * ctx, chans, cols), CTX + ("zh",), split_axis=0, concat_axis=0, tiled=True
    ).reshape(ctx, 2, chans, cols)
    other = turned(own, "core", 1)
    return project(place, other, weight, project(place, own, weight))


def solution(mesh):
    fine = Mesh(mesh.devices.reshape(4, 4, 4, 2, 2), ("y", "x", "zl", "zh", "core"))
    mp = ("zh", "core")
    return jax.shard_map(
        shards,
        mesh=fine,
        in_specs=(
            P(mp, CTX),
            P(mp, CTX),
            P(mp, CTX),
            P(None, mp, None),
            P(mp + CTX, None),
            P(mp + CTX),
            P(CTX, mp),
        ),
        out_specs=P(mp, CTX),
        check_vma=False,
    )
```

```python
import math

import jax
import jax.numpy as jnp
import numpy as np
from jax import lax
from jax.experimental import pallas as pl
from jax.experimental.pallas import tpu as pltpu
from jax.sharding import Mesh, PartitionSpec as P

BF16 = jnp.bfloat16
F32 = jnp.float32
CTX = ("y", "x", "zl")
MIB = 1024 * 1024
VMEM_LIMIT = 60 * MIB


def hi_lo(table):
    hi = table.astype(np.float32).astype(jnp.bfloat16)
    lo = (table - hi.astype(np.float64)).astype(np.float32).astype(jnp.bfloat16)
    return hi, lo


def dft_tables(outer, inner):
    length = outer * inner
    freq = np.arange(outer)[:, None] + 0.25
    angle = 2.0 * np.pi * freq * np.arange(outer)[None, :] / outer
    first = np.concatenate([np.cos(angle), -np.sin(angle)], axis=0)
    spin = 2.0 * np.pi * freq * np.arange(inner)[None, :] / length
    steps = np.outer(np.arange(inner), np.arange(inner)) % inner
    turn = 2.0 * np.pi * steps / inner
    cos, sin = np.cos(turn), np.sin(turn)
    second = np.block([[cos, -sin], [sin, cos]])
    return {
        "first": hi_lo(first),
        "last": hi_lo(first.T.copy()),
        "spin": (np.cos(spin).astype(np.float32), np.sin(spin).astype(np.float32)),
        "second": hi_lo(second),
    }


def dot(left, right):
    return jnp.dot(left, right, preferred_element_type=F32)


def split_bf16(value):
    hi = value.astype(BF16)
    return hi, (value - hi.astype(F32)).astype(BF16)


def lane_ids(rows):
    return lax.broadcasted_iota(jnp.int32, (rows, 128), 1)


def filter_tiles(weights, before, tiles, lane):
    turned = {}
    for tap in range(1, len(weights)):
        for index, tile in enumerate(tiles):
            turned[index, tap] = pltpu.roll(tile, tap, 1)
        turned[-1, tap] = 0.0 if before is None else pltpu.roll(before, tap, 1)
    sums = []
    for index, tile in enumerate(tiles):
        total = weights[0] * tile
        for tap in range(1, len(weights)):
            total += weights[tap] * jnp.where(lane >= tap, turned[index, tap], turned[index - 1, tap])
        sums.append(total)
    return sums


def short_kernel(taps_ref, q_ref, k_ref, v_ref, out_ref):
    rows, cols = q_ref.shape
    taps = taps_ref.shape[1]
    size = out_ref.shape[1]
    first = pl.program_id(0) * (rows // size)
    lane = lane_ids(size)
    for g in range(rows // size):
        at = pl.ds(g * size, size)
        feats, edges = [], []
        for index, ref in ((1, k_ref), (2, v_ref)):
            wide = ref[at, :].astype(F32)
            tiles = [wide[:, i * 128 : i * 128 + 128] for i in range(cols // 128)]
            weights = [taps_ref[index, tap, first + g] for tap in range(taps)]
            feats.append(filter_tiles(weights, None, tiles, lane))
            shift = 8 if index == 1 else 24
            edges += [pltpu.roll(tiles[-1], shift, 1), pltpu.roll(tiles[0], shift, 1)]
        for i in range(cols // 128):
            out_ref[g, :, i * 128 : i * 128 + 128] = (feats[0][i] * feats[1][i]).astype(BF16)
        out_ref[g, :, cols : 2 * cols] = q_ref[at, :]
        edge = jnp.where(lane < 16, jnp.where(lane < 8, edges[0], edges[1]), jnp.where(lane < 24, edges[2], edges[3]))
        out_ref[g, :, 2 * cols :] = edge.astype(BF16)


def short_filters(taps, query, key, value, ctx, blocks=4):
    rows, cols = query.shape
    size = rows // ctx
    spec = pl.BlockSpec((rows // blocks, cols), lambda i: (i, 0))
    return pl.pallas_call(
        short_kernel,
        grid=(blocks,),
        in_specs=[pl.BlockSpec(memory_space=pltpu.SMEM)] + [spec] * 3,
        out_specs=pl.BlockSpec((ctx // blocks, size, 2 * cols + 128), lambda i: (i, 0, 0)),
        out_shape=jax.ShapeDtypeStruct((ctx, size, 2 * cols + 128), BF16),
        compiler_params=pltpu.CompilerParams(vmem_limit_bytes=VMEM_LIMIT),
        cost_estimate=pl.CostEstimate(flops=2 * 14 * rows * cols, bytes_accessed=10 * rows * cols, transcendentals=0),
        name="short_filters",
    )(taps, query, key, value)


def second_dft(hi, lo, second_hi, second_lo):
    return dot(hi, second_hi[...]) + dot(lo, second_hi[...]) + dot(hi, second_lo[...])


def channel_rows(ref, c, outer, chans):
    halves = ref.shape[0] // (outer * chans)
    parts = [ref[pl.ds(half * outer * chans + c, outer, stride=chans), :] for half in range(halves)]
    return jnp.concatenate(parts, axis=1)


def filter_kernel(scale, filt_ref, f_hi, f_lo, cos_ref, sin_ref, s_hi, s_lo, out_ref, rows_ref, g_hi, g_lo):
    chans, _ = filt_ref.shape
    outer, inner = cos_ref.shape
    for half in range(inner // 128):
        for a in range(outer):
            start = a * inner + half * 128
            at = (half * outer + a) * chans
            rows_ref[at : at + chans, :] = filt_ref[:, start : start + 128]

    for c in range(chans):
        hi, lo = split_bf16(channel_rows(rows_ref, c, outer, chans) * scale)
        mixed = dot(f_hi[...], hi) + dot(f_hi[...], lo) + dot(f_lo[...], hi)
        re, im = mixed[:outer], mixed[outer:]
        at = pl.ds(c * outer, outer)
        g_hi[at, :inner], g_lo[at, :inner] = split_bf16(re * cos_ref[...] + im * sin_ref[...])
        g_hi[at, inner:], g_lo[at, inner:] = split_bf16(im * cos_ref[...] - re * sin_ref[...])

    for i in range(chans * outer // 256):
        at = pl.ds(i * 256, 256)
        out_ref[at, :] = second_dft(g_hi[at, :], g_lo[at, :], s_hi, s_lo)


def filter_spectrum(long_filter, tables, outer, inner):
    chans = long_filter.shape[0]
    rows = chans * outer
    whole = lambda shape: pl.BlockSpec(shape, lambda i: (0,) * len(shape))
    operands = (long_filter, *tables["first"], *tables["spin"], *tables["second"])
    return pl.pallas_call(
        lambda *refs: filter_kernel(1.0 / (outer * inner), *refs),
        grid=(1,),
        in_specs=[whole(operand.shape) for operand in operands],
        out_specs=whole((rows, 2 * inner)),
        out_shape=jax.ShapeDtypeStruct((rows, 2 * inner), F32),
        scratch_shapes=[
            pltpu.VMEM((rows * inner // 128, 128), F32),
            pltpu.VMEM((rows, 2 * inner), BF16),
            pltpu.VMEM((rows, 2 * inner), BF16),
        ],
        compiler_params=pltpu.CompilerParams(vmem_limit_bytes=VMEM_LIMIT),
        cost_estimate=pl.CostEstimate(flops=3 * 2 * rows * 4 * inner * inner, bytes_accessed=5 * 2**20, transcendentals=0),
        name="filter_spectrum",
    )(*operands)


def conv_kernel(
    place_ref, skip_ref, taps_ref, in_ref, f_hi, f_lo, l_hi, l_lo, cos_ref, sin_ref, spec_hbm, s_hi_hbm, s_lo_hbm,
    out_ref, rows_ref, z_ref, q_ref, edge_ref, g_hi, g_lo, spec_ref, s_hi, s_lo, sems,
):
    fetches = [
        pltpu.make_async_copy(source, target, sems.at[index])
        for index, (source, target) in enumerate(((spec_hbm, spec_ref), (s_hi_hbm, s_hi), (s_lo_hbm, s_lo)))
    ]
    for fetch in fetches:
        fetch.start()
    outer, chans, width = in_ref.shape
    inner = (width - 128) // 2
    halves = inner // 128
    rows = outer * chans
    taps = taps_ref.shape[1]
    group = place_ref[0]
    blocks = 8
    step = rows // blocks
    units = outer // blocks
    lane = lane_ids(step)

    edge_ref[:chans, :] = jnp.zeros((chans, 128), F32)
    q_ref[(halves - 1) * (rows + chans) : (halves - 1) * (rows + chans) + chans, :] = jnp.zeros((chans, 128), F32)
    edge_ref[chans:, :] = in_ref[:, :, 2 * inner :].reshape(rows, 128).astype(F32)
    for half in range(halves):
        at = half * (rows + chans) + chans
        q_ref[at : at + rows, :] = (
            in_ref[:, :, inner + half * 128 : inner + half * 128 + 128].reshape(rows, 128).astype(F32)
        )

    weights = [jnp.where(lane < 16, taps_ref[1, tap, group], taps_ref[2, tap, group]) for tap in range(taps)]

    for i in range(blocks):
        at = i * step
        edge = jnp.where(jnp.bitwise_and(lane, 8) == 0, edge_ref[at : at + step, :], edge_ref[at + chans : at + chans + step, :])
        total = weights[0] * edge
        for tap in range(1, taps):
            total += weights[tap] * pltpu.roll(edge, tap, 1)
        first = (pltpu.roll(total, 120, 1) * pltpu.roll(total, 104, 1)).astype(BF16).astype(F32)
        sig = in_ref[i * units : (i + 1) * units, :, :inner].reshape(step, inner).astype(F32)
        rows_ref[at : at + step, :] = jnp.where(lane < taps - 1, first, sig[:, :128])
        for half in range(1, halves):
            rows_ref[half * rows + at : half * rows + at + step, :] = sig[:, half * 128 : half * 128 + 128]

    for c in range(chans):
        sig = channel_rows(rows_ref, c, outer, chans).astype(BF16)
        mixed = dot(f_hi[...], sig) + dot(f_lo[...], sig)
        re, im = mixed[:outer], mixed[outer:]
        at = pl.ds(c * outer, outer)
        g_hi[at, :inner], g_lo[at, :inner] = split_bf16(re * cos_ref[...] + im * sin_ref[...])
        g_hi[at, inner:], g_lo[at, inner:] = split_bf16(im * cos_ref[...] - re * sin_ref[...])

    for fetch in fetches:
        fetch.wait()

    block = min(chans * outer, 512)
    for i in range(chans * outer // block):
        at = pl.ds(i * block, block)
        sig = second_dft(g_hi[at, :], g_lo[at, :], s_hi, s_lo)
        sr, si = sig[:, :inner], sig[:, inner:]
        hr, hm = spec_ref[at, :inner], spec_ref[at, inner:]
        r_hi, r_lo = split_bf16(sr * hr - si * hm)
        i_hi, i_lo = split_bf16(-(sr * hm + si * hr))
        back = second_dft(
            jnp.concatenate([r_hi, i_hi], axis=1), jnp.concatenate([r_lo, i_lo], axis=1), s_hi, s_lo
        )
        back = back.reshape(block // outer, outer, 2 * inner)
        re, im = back[:, :, :inner], back[:, :, inner:]
        cos, sin = cos_ref[...], sin_ref[...]
        r_hi, r_lo = split_bf16((re * cos + im * sin).reshape(block, inner))
        i_hi, i_lo = split_bf16((re * sin - im * cos).reshape(block, inner))
        for j in range(block // outer):
            c = i * (block // outer) + j
            part = slice(j * outer, (j + 1) * outer)
            hi = jnp.concatenate([r_hi[part], i_hi[part]], axis=0)
            lo = jnp.concatenate([r_lo[part], i_lo[part]], axis=0)
            conv = dot(l_hi[...], hi) + dot(l_hi[...], lo) + dot(l_lo[...], hi)
            mixed = conv + skip_ref[c] * channel_rows(rows_ref, c, outer, chans)
            for half in range(halves):
                z_ref[pl.ds(half * rows + c, outer, stride=chans), :] = mixed[:, half * 128 : (half + 1) * 128]

    q_taps = [taps_ref[0, tap, group] for tap in range(taps)]
    for i in range(blocks):
        at = i * step
        starts = [half * (rows + chans) + chans + at for half in range(halves)]
        tiles = [q_ref[start : start + step, :] for start in starts]
        start = (halves - 1) * (rows + chans) + at
        feats = filter_tiles(q_taps, q_ref[start : start + step, :], tiles, lane)
        for half in range(halves):
            mixed = z_ref[half * rows + at : half * rows + at + step, :].astype(BF16).astype(F32)
            result = (feats[half] * mixed).astype(BF16).reshape(units, chans, 128)
            for copy in range(out_ref.shape[1]):
                out_ref[i * units : (i + 1) * units, copy, :, half * 128 : (half + 1) * 128] = result


def long_mix(place, arrived, spectrum, skip_bias, taps, tables, copies):
    outer, chans, width = arrived.shape
    inner = (width - 128) // 2
    rows = outer * chans
    whole = lambda shape: pl.BlockSpec(shape, lambda i: (0,) * len(shape))
    scalars = pl.BlockSpec(memory_space=pltpu.SMEM)
    operands = (arrived, *tables["first"], *tables["last"], *tables["spin"])
    fetched = (spectrum, *tables["second"])
    return pl.pallas_call(
        conv_kernel,
        grid=(1,),
        in_specs=[scalars] * 3
        + [whole(operand.shape) for operand in operands]
        + [pl.BlockSpec(memory_space=pl.ANY)] * len(fetched),
        out_specs=whole((outer, copies, chans, inner)),
        out_shape=jax.ShapeDtypeStruct((outer, copies, chans, inner), BF16),
        scratch_shapes=[
            pltpu.VMEM((rows * inner // 128, 128), F32),
            pltpu.VMEM((rows * inner // 128, 128), F32),
            pltpu.VMEM(((rows + chans) * inner // 128, 128), F32),
            pltpu.VMEM((rows + chans, 128), F32),
            pltpu.VMEM((rows, 2 * inner), BF16),
            pltpu.VMEM((rows, 2 * inner), BF16),
            pltpu.VMEM((rows, 2 * inner), F32),
            pltpu.VMEM((2 * inner, 2 * inner), BF16),
            pltpu.VMEM((2 * inner, 2 * inner), BF16),
            pltpu.SemaphoreType.DMA((3,)),
        ],
        compiler_params=pltpu.CompilerParams(vmem_limit_bytes=VMEM_LIMIT),
        cost_estimate=pl.CostEstimate(flops=2**20, bytes_accessed=2**20, transcendentals=0),
        name="long_conv",
    )(place, skip_bias, taps, *operands, *fetched)


def project_kernel(other, place_ref, z_hbm, *refs):
    by_y, by_x, refs = refs[:4], refs[4:8], refs[8:]
    if other:
        sum_hbm, out_hbm, z_ref, w_ref, g_ref, out_ref, sum_ref, sems = refs
    else:
        out_hbm, z_ref, w_ref, g_ref, out_ref, sems = refs
    _, halves, chans, cols = z_ref.shape
    depth, width = w_ref.shape
    unit = 4 * chans
    size = 4 * unit
    run = size // 2
    block = 256
    zl, y, x_here = place_ref[1], place_ref[4], place_ref[5]
    core = jnp.bitwise_xor(place_ref[3], other)

    def copy(source, target, index):
        fetch = pltpu.make_async_copy(source, target, sems.at[index])
        fetch.start()
        return fetch

    arriving = copy(z_hbm, z_ref, 0)
    fetches = []
    for half in range(halves):
        for x in range(4):
            index = half * 4 + x
            along_y = jnp.bitwise_and(y - (half * 2 + core), 3)
            along_x = jnp.bitwise_and(x_here - x, 3)
            for part, (held, pick, row) in enumerate(((by_y, along_y, along_x), (by_x, along_x, along_y))):
                source = pl.ds(pl.multiple_of(row * run, run), run)
                target = w_ref.at[pl.ds(index * size + part * run, run)]
                sem = 1 + 2 * index + part
                for turn in range(4):

                    @pl.when(pick == turn)
                    def _():
                        copy(held[turn].at[source], target, sem)

                fetches.append(pltpu.make_async_copy(held[0].at[source], target, sems.at[sem]))
    if other:
        fetches.append(copy(sum_hbm, sum_ref, 17))
    arriving.wait()
    for half in range(halves):
        for x in range(4):
            parts = []
            for turn in range(4):
                start = x * 16 + 4 * jnp.bitwise_and(zl - turn, 3)
                parts.append(z_ref[pl.ds(start, 4), half].reshape(unit, cols))
            to = (half * 4 + x) * size
            g_ref[:, to : to + size] = jnp.concatenate(parts, axis=0).T
    for fetch in fetches:
        fetch.wait()
    leaving = []
    for index in range(width // block):
        at = slice(index * block, (index + 1) * block)
        part = dot(g_ref[...], w_ref[:, at])
        if other:
            out_ref[at, :] = (part + sum_ref[:, at]).T.astype(BF16)
            leaving.append(copy(out_ref.at[at], out_hbm.at[at], 18 + index))
        else:
            out_ref[index] = part
            leaving.append(copy(out_ref.at[index], out_hbm.at[:, at], 18 + index))
    for leave in leaving:
        leave.wait()


def project(place, gated, weight, partial=None):
    width = weight[0].shape[1]
    depth = 4 * weight[0].shape[0]
    cols = gated.shape[3]
    other = 0 if partial is None else 1
    anywhere = pl.BlockSpec(memory_space=pl.ANY)
    operands = [gated, *weight] + ([partial] if other else [])
    shape = (width, cols) if other else (cols, width)
    return pl.pallas_call(
        lambda *refs: project_kernel(other, *refs),
        in_specs=[pl.BlockSpec(memory_space=pltpu.SMEM)] + [anywhere] * len(operands),
        out_specs=anywhere,
        out_shape=jax.ShapeDtypeStruct(shape, BF16 if other else F32),
        scratch_shapes=[
            pltpu.VMEM(gated.shape, BF16),
            pltpu.VMEM((depth, width), BF16),
            pltpu.VMEM((cols, depth), BF16),
            pltpu.VMEM(shape, BF16) if other else pltpu.VMEM((width // 256, cols, 256), F32),
        ]
        + ([pltpu.VMEM((cols, width), F32)] if other else [])
        + [pltpu.SemaphoreType.DMA((18 + width // 256,))],
        compiler_params=pltpu.CompilerParams(vmem_limit_bytes=VMEM_LIMIT - 12 * MIB),
        cost_estimate=pl.CostEstimate(flops=2 * depth * width * cols, bytes_accessed=2 * depth * width, transcendentals=0),
        name="project_last" if other else "project_first",
    )(place, *operands)


def turned(value, axis, steps):
    count = lax.axis_size(axis)
    return lax.ppermute(value, axis, [(source, (source + steps) % count) for source in range(count)])


def shards(query_proj, key_proj, value_proj, short_taps, long_filter, skip_bias, out_weight):
    rows, cols = query_proj.shape
    ctx = lax.axis_size(CTX)
    chans = long_filter.shape[0]
    tables = dft_tables(ctx, cols)

    taps = jnp.swapaxes(short_taps, 1, 2)
    place = jnp.stack([lax.axis_index(name) for name in (CTX, "zl", "zh", "core", "y", "x")]).astype(jnp.int32)

    pieces = [turned(out_weight, "zl", step) for step in (1, 2, 3)]
    ready = short_filters(taps, query_proj, key_proj, value_proj, ctx)
    arrived = lax.all_to_all(ready, CTX, split_axis=0, concat_axis=0, tiled=True)

    first_half = jnp.concatenate([out_weight, pieces[0]], axis=0)
    second_half = jnp.concatenate(pieces[1:], axis=0)
    run_x = jnp.concatenate([first_half] + [turned(first_half, "x", step) for step in (1, 2, 3)], axis=0)
    run_y = jnp.concatenate([second_half] + [turned(second_half, "y", step) for step in (1, 2, 3)], axis=0)
    near = [turned(run_x, "y", 1), turned(run_x, "y", 3), turned(run_y, "x", 1), turned(run_y, "x", 3)]

    long_filter, run_x, run_y = lax.optimization_barrier((long_filter, run_x, run_y))
    spectrum = filter_spectrum(long_filter, tables, ctx, cols)
    gated = long_mix(place, arrived, spectrum, skip_bias, taps, tables, 2)
    gated, run_x, run_y, *near = lax.optimization_barrier((gated, run_x, run_y, *near))
    by_y = [run_x, near[0], turned(run_x, "y", 2), near[1]]
    by_x = [run_y, near[2], turned(run_y, "x", 2), near[3]]
    weight = by_y + by_x

    own = lax.all_to_all(
        gated.reshape(2 * ctx, chans, cols), CTX + ("zh",), split_axis=0, concat_axis=0, tiled=True
    ).reshape(ctx, 2, chans, cols)
    other = turned(own, "core", 1)
    return project(place, other, weight, project(place, own, weight))


def solution(mesh):
    fine = Mesh(mesh.devices.reshape(4, 4, 4, 2, 2), ("y", "x", "zl", "zh", "core"))
    mp = ("zh", "core")
    return jax.shard_map(
        shards,
        mesh=fine,
        in_specs=(
            P(mp, CTX),
            P(mp, CTX),
            P(mp, CTX),
            P(None, mp, None),
            P(mp + CTX, None),
            P(mp + CTX),
            P(CTX, mp),
        ),
        out_specs=P(mp, CTX),
        check_vma=False,
    )
```

```python
import math

import jax
import jax.numpy as jnp
import numpy as np
from jax import lax
from jax.experimental import pallas as pl
from jax.experimental.pallas import tpu as pltpu
from jax.sharding import Mesh, PartitionSpec as P

BF16 = jnp.bfloat16
F32 = jnp.float32
CTX = ("y", "x", "zl")
MIB = 1024 * 1024
VMEM_LIMIT = 60 * MIB


def hi_lo(table):
    hi = table.astype(np.float32).astype(jnp.bfloat16)
    lo = (table - hi.astype(np.float64)).astype(np.float32).astype(jnp.bfloat16)
    return hi, lo


def dft_tables(outer, inner):
    length = outer * inner
    freq = np.arange(outer)[:, None] + 0.25
    angle = 2.0 * np.pi * freq * np.arange(outer)[None, :] / outer
    first = np.concatenate([np.cos(angle), -np.sin(angle)], axis=0)
    spin = 2.0 * np.pi * freq * np.arange(inner)[None, :] / length
    steps = np.outer(np.arange(inner), np.arange(inner)) % inner
    turn = 2.0 * np.pi * steps / inner
    cos, sin = np.cos(turn), np.sin(turn)
    second = np.block([[cos, -sin], [sin, cos]])
    return {
        "first": hi_lo(first),
        "last": hi_lo(first.T.copy()),
        "spin": (np.cos(spin).astype(np.float32), np.sin(spin).astype(np.float32)),
        "second": hi_lo(second),
    }


def dot(left, right):
    return jnp.dot(left, right, preferred_element_type=F32)


def split_bf16(value):
    hi = value.astype(BF16)
    return hi, (value - hi.astype(F32)).astype(BF16)


def lane_ids(rows):
    return lax.broadcasted_iota(jnp.int32, (rows, 128), 1)


def filter_tiles(weights, before, tiles, lane):
    turned = {}
    for tap in range(1, len(weights)):
        for index, tile in enumerate(tiles):
            turned[index, tap] = pltpu.roll(tile, tap, 1)
        turned[-1, tap] = 0.0 if before is None else pltpu.roll(before, tap, 1)
    sums = []
    for index, tile in enumerate(tiles):
        total = weights[0] * tile
        for tap in range(1, len(weights)):
            total += weights[tap] * jnp.where(lane >= tap, turned[index, tap], turned[index - 1, tap])
        sums.append(total)
    return sums


def short_kernel(taps_ref, q_ref, k_ref, v_ref, out_ref):
    rows, cols = q_ref.shape
    taps = taps_ref.shape[1]
    size = out_ref.shape[1]
    first = pl.program_id(0) * (rows // size)
    lane = lane_ids(size)
    for g in range(rows // size):
        at = pl.ds(g * size, size)
        feats, edges = [], []
        for index, ref in ((1, k_ref), (2, v_ref)):
            wide = ref[at, :].astype(F32)
            tiles = [wide[:, i * 128 : i * 128 + 128] for i in range(cols // 128)]
            weights = [taps_ref[index, tap, first + g] for tap in range(taps)]
            feats.append(filter_tiles(weights, None, tiles, lane))
            shift = 8 if index == 1 else 24
            edges += [pltpu.roll(tiles[-1], shift, 1), pltpu.roll(tiles[0], shift, 1)]
        for i in range(cols // 128):
            out_ref[g, :, i * 128 : i * 128 + 128] = (feats[0][i] * feats[1][i]).astype(BF16)
        out_ref[g, :, cols : 2 * cols] = q_ref[at, :]
        edge = jnp.where(lane < 16, jnp.where(lane < 8, edges[0], edges[1]), jnp.where(lane < 24, edges[2], edges[3]))
        out_ref[g, :, 2 * cols :] = edge.astype(BF16)


def short_filters(taps, query, key, value, ctx, blocks=4):
    rows, cols = query.shape
    size = rows // ctx
    spec = pl.BlockSpec((rows // blocks, cols), lambda i: (i, 0))
    return pl.pallas_call(
        short_kernel,
        grid=(blocks,),
        in_specs=[pl.BlockSpec(memory_space=pltpu.SMEM)] + [spec] * 3,
        out_specs=pl.BlockSpec((ctx // blocks, size, 2 * cols + 128), lambda i: (i, 0, 0)),
        out_shape=jax.ShapeDtypeStruct((ctx, size, 2 * cols + 128), BF16),
        compiler_params=pltpu.CompilerParams(vmem_limit_bytes=VMEM_LIMIT),
        cost_estimate=pl.CostEstimate(flops=2 * 14 * rows * cols, bytes_accessed=10 * rows * cols, transcendentals=0),
        name="short_filters",
    )(taps, query, key, value)


def second_dft(hi, lo, second_hi, second_lo):
    return dot(hi, second_hi[...]) + dot(lo, second_hi[...]) + dot(hi, second_lo[...])


def channel_rows(ref, c, outer, chans):
    halves = ref.shape[0] // (outer * chans)
    parts = [ref[pl.ds(half * outer * chans + c, outer, stride=chans), :] for half in range(halves)]
    return jnp.concatenate(parts, axis=1)


def filter_kernel(scale, filt_ref, f_hi, f_lo, cos_ref, sin_ref, s_hi, s_lo, out_ref, rows_ref, g_hi, g_lo):
    chans, _ = filt_ref.shape
    outer, inner = cos_ref.shape
    for half in range(inner // 128):
        for a in range(outer):
            start = a * inner + half * 128
            at = (half * outer + a) * chans
            rows_ref[at : at + chans, :] = filt_ref[:, start : start + 128]

    for c in range(chans):
        hi, lo = split_bf16(channel_rows(rows_ref, c, outer, chans) * scale)
        mixed = dot(f_hi[...], hi) + dot(f_hi[...], lo) + dot(f_lo[...], hi)
        re, im = mixed[:outer], mixed[outer:]
        at = pl.ds(c * outer, outer)
        g_hi[at, :inner], g_lo[at, :inner] = split_bf16(re * cos_ref[...] + im * sin_ref[...])
        g_hi[at, inner:], g_lo[at, inner:] = split_bf16(im * cos_ref[...] - re * sin_ref[...])

    for i in range(chans * outer // 256):
        at = pl.ds(i * 256, 256)
        out_ref[at, :] = second_dft(g_hi[at, :], g_lo[at, :], s_hi, s_lo)


def filter_spectrum(long_filter, tables, outer, inner):
    chans = long_filter.shape[0]
    rows = chans * outer
    whole = lambda shape: pl.BlockSpec(shape, lambda i: (0,) * len(shape))
    operands = (long_filter, *tables["first"], *tables["spin"], *tables["second"])
    return pl.pallas_call(
        lambda *refs: filter_kernel(1.0 / (outer * inner), *refs),
        grid=(1,),
        in_specs=[whole(operand.shape) for operand in operands],
        out_specs=whole((rows, 2 * inner)),
        out_shape=jax.ShapeDtypeStruct((rows, 2 * inner), F32),
        scratch_shapes=[
            pltpu.VMEM((rows * inner // 128, 128), F32),
            pltpu.VMEM((rows, 2 * inner), BF16),
            pltpu.VMEM((rows, 2 * inner), BF16),
        ],
        compiler_params=pltpu.CompilerParams(vmem_limit_bytes=VMEM_LIMIT),
        cost_estimate=pl.CostEstimate(flops=3 * 2 * rows * 4 * inner * inner, bytes_accessed=5 * 2**20, transcendentals=0),
        name="filter_spectrum",
    )(*operands)


def conv_kernel(
    place_ref, skip_ref, taps_ref, in_ref, f_hi, f_lo, l_hi, l_lo, cos_ref, sin_ref, spec_hbm, s_hi_hbm, s_lo_hbm,
    out_ref, rows_ref, z_ref, q_ref, edge_ref, g_hi, g_lo, spec_ref, s_hi, s_lo, sems,
):
    fetches = [
        pltpu.make_async_copy(source, target, sems.at[index])
        for index, (source, target) in enumerate(((spec_hbm, spec_ref), (s_hi_hbm, s_hi), (s_lo_hbm, s_lo)))
    ]
    for fetch in fetches:
        fetch.start()
    outer, chans, width = in_ref.shape
    inner = (width - 128) // 2
    halves = inner // 128
    rows = outer * chans
    taps = taps_ref.shape[1]
    group = place_ref[0]
    blocks = 8
    step = rows // blocks
    units = outer // blocks
    lane = lane_ids(step)

    edge_ref[:chans, :] = jnp.zeros((chans, 128), F32)
    q_ref[(halves - 1) * (rows + chans) : (halves - 1) * (rows + chans) + chans, :] = jnp.zeros((chans, 128), F32)
    edge_ref[chans:, :] = in_ref[:, :, 2 * inner :].reshape(rows, 128).astype(F32)
    for half in range(halves):
        at = half * (rows + chans) + chans
        q_ref[at : at + rows, :] = (
            in_ref[:, :, inner + half * 128 : inner + half * 128 + 128].reshape(rows, 128).astype(F32)
        )

    weights = [jnp.where(lane < 16, taps_ref[1, tap, group], taps_ref[2, tap, group]) for tap in range(taps)]

    for i in range(blocks):
        at = i * step
        edge = jnp.where(jnp.bitwise_and(lane, 8) == 0, edge_ref[at : at + step, :], edge_ref[at + chans : at + chans + step, :])
        total = weights[0] * edge
        for tap in range(1, taps):
            total += weights[tap] * pltpu.roll(edge, tap, 1)
        first = (pltpu.roll(total, 120, 1) * pltpu.roll(total, 104, 1)).astype(BF16).astype(F32)
        sig = in_ref[i * units : (i + 1) * units, :, :inner].reshape(step, inner).astype(F32)
        rows_ref[at : at + step, :] = jnp.where(lane < taps - 1, first, sig[:, :128])
        for half in range(1, halves):
            rows_ref[half * rows + at : half * rows + at + step, :] = sig[:, half * 128 : half * 128 + 128]

    for c in range(chans):
        sig = channel_rows(rows_ref, c, outer, chans).astype(BF16)
        mixed = dot(f_hi[...], sig) + dot(f_lo[...], sig)
        re, im = mixed[:outer], mixed[outer:]
        at = pl.ds(c * outer, outer)
        g_hi[at, :inner], g_lo[at, :inner] = split_bf16(re * cos_ref[...] + im * sin_ref[...])
        g_hi[at, inner:], g_lo[at, inner:] = split_bf16(im * cos_ref[...] - re * sin_ref[...])

    for fetch in fetches:
        fetch.wait()

    block = min(chans * outer, 512)
    for i in range(chans * outer // block):
        at = pl.ds(i * block, block)
        sig = second_dft(g_hi[at, :], g_lo[at, :], s_hi, s_lo)
        sr, si = sig[:, :inner], sig[:, inner:]
        hr, hm = spec_ref[at, :inner], spec_ref[at, inner:]
        r_hi, r_lo = split_bf16(sr * hr - si * hm)
        i_hi, i_lo = split_bf16(-(sr * hm + si * hr))
        back = second_dft(
            jnp.concatenate([r_hi, i_hi], axis=1), jnp.concatenate([r_lo, i_lo], axis=1), s_hi, s_lo
        )
        back = back.reshape(block // outer, outer, 2 * inner)
        re, im = back[:, :, :inner], back[:, :, inner:]
        cos, sin = cos_ref[...], sin_ref[...]
        r_hi, r_lo = split_bf16((re * cos + im * sin).reshape(block, inner))
        i_hi, i_lo = split_bf16((re * sin - im * cos).reshape(block, inner))
        for j in range(block // outer):
            c = i * (block // outer) + j
            part = slice(j * outer, (j + 1) * outer)
            hi = jnp.concatenate([r_hi[part], i_hi[part]], axis=0)
            lo = jnp.concatenate([r_lo[part], i_lo[part]], axis=0)
            conv = dot(l_hi[...], hi) + dot(l_hi[...], lo) + dot(l_lo[...], hi)
            mixed = conv + skip_ref[c] * channel_rows(rows_ref, c, outer, chans)
            for half in range(halves):
                z_ref[pl.ds(half * rows + c, outer, stride=chans), :] = mixed[:, half * 128 : (half + 1) * 128]

    q_taps = [taps_ref[0, tap, group] for tap in range(taps)]
    for i in range(blocks):
        at = i * step
        starts = [half * (rows + chans) + chans + at for half in range(halves)]
        tiles = [q_ref[start : start + step, :] for start in starts]
        start = (halves - 1) * (rows + chans) + at
        feats = filter_tiles(q_taps, q_ref[start : start + step, :], tiles, lane)
        for half in range(halves):
            mixed = z_ref[half * rows + at : half * rows + at + step, :].astype(BF16).astype(F32)
            result = (feats[half] * mixed).astype(BF16).reshape(units, chans, 128)
            for copy in range(out_ref.shape[1]):
                out_ref[i * units : (i + 1) * units, copy, :, half * 128 : (half + 1) * 128] = result


def long_mix(place, arrived, spectrum, skip_bias, taps, tables, copies):
    outer, chans, width = arrived.shape
    inner = (width - 128) // 2
    rows = outer * chans
    whole = lambda shape: pl.BlockSpec(shape, lambda i: (0,) * len(shape))
    scalars = pl.BlockSpec(memory_space=pltpu.SMEM)
    operands = (arrived, *tables["first"], *tables["last"], *tables["spin"])
    fetched = (spectrum, *tables["second"])
    return pl.pallas_call(
        conv_kernel,
        grid=(1,),
        in_specs=[scalars] * 3
        + [whole(operand.shape) for operand in operands]
        + [pl.BlockSpec(memory_space=pl.ANY)] * len(fetched),
        out_specs=whole((outer, copies, chans, inner)),
        out_shape=jax.ShapeDtypeStruct((outer, copies, chans, inner), BF16),
        scratch_shapes=[
            pltpu.VMEM((rows * inner // 128, 128), F32),
            pltpu.VMEM((rows * inner // 128, 128), F32),
            pltpu.VMEM(((rows + chans) * inner // 128, 128), F32),
            pltpu.VMEM((rows + chans, 128), F32),
            pltpu.VMEM((rows, 2 * inner), BF16),
            pltpu.VMEM((rows, 2 * inner), BF16),
            pltpu.VMEM((rows, 2 * inner), F32),
            pltpu.VMEM((2 * inner, 2 * inner), BF16),
            pltpu.VMEM((2 * inner, 2 * inner), BF16),
            pltpu.SemaphoreType.DMA((3,)),
        ],
        compiler_params=pltpu.CompilerParams(vmem_limit_bytes=VMEM_LIMIT),
        cost_estimate=pl.CostEstimate(flops=2**20, bytes_accessed=2**20, transcendentals=0),
        name="long_conv",
    )(place, skip_bias, taps, *operands, *fetched)


def project_kernel(other, place_ref, z_hbm, *refs):
    by_y, by_x, refs = refs[:4], refs[4:8], refs[8:]
    if other:
        sum_hbm, out_hbm, z_ref, w_ref, g_ref, out_ref, sum_ref, sems = refs
    else:
        out_hbm, z_ref, w_ref, g_ref, out_ref, sems = refs
    _, halves, chans, cols = z_ref.shape
    depth, width = w_ref.shape
    unit = 4 * chans
    size = 4 * unit
    run = size // 2
    block = 256
    zl, y, x_here = place_ref[1], place_ref[4], place_ref[5]
    core = jnp.bitwise_xor(place_ref[3], other)

    def copy(source, target, index):
        fetch = pltpu.make_async_copy(source, target, sems.at[index])
        fetch.start()
        return fetch

    arriving = copy(z_hbm, z_ref, 0)
    fetches = []
    for half in range(halves):
        for x in range(4):
            index = half * 4 + x
            along_y = jnp.bitwise_and(y - (half * 2 + core), 3)
            along_x = jnp.bitwise_and(x_here - x, 3)
            for part, (held, pick, row) in enumerate(((by_y, along_y, along_x), (by_x, along_x, along_y))):
                source = pl.ds(pl.multiple_of(row * run, run), run)
                target = w_ref.at[pl.ds(index * size + part * run, run)]
                sem = 1 + 2 * index + part
                for turn in range(4):

                    @pl.when(pick == turn)
                    def _():
                        copy(held[turn].at[source], target, sem)

                fetches.append(pltpu.make_async_copy(held[0].at[source], target, sems.at[sem]))
    if other:
        fetches.append(copy(sum_hbm, sum_ref, 17))
    arriving.wait()
    for half in range(halves):
        for x in range(4):
            parts = []
            for turn in range(4):
                start = x * 16 + 4 * jnp.bitwise_and(zl - turn, 3)
                parts.append(z_ref[pl.ds(start, 4), half].reshape(unit, cols))
            to = (half * 4 + x) * size
            g_ref[:, to : to + size] = jnp.concatenate(parts, axis=0).T
    for fetch in fetches:
        fetch.wait()
    leaving = []
    for index in range(width // block):
        at = slice(index * block, (index + 1) * block)
        part = dot(g_ref[...], w_ref[:, at])
        if other:
            out_ref[at, :] = (part + sum_ref[:, at]).T.astype(BF16)
            leaving.append(copy(out_ref.at[at], out_hbm.at[at], 18 + index))
        else:
            out_ref[index] = part
            leaving.append(copy(out_ref.at[index], out_hbm.at[:, at], 18 + index))
    for leave in leaving:
        leave.wait()


def project(place, gated, weight, partial=None):
    width = weight[0].shape[1]
    depth = 4 * weight[0].shape[0]
    cols = gated.shape[3]
    other = 0 if partial is None else 1
    anywhere = pl.BlockSpec(memory_space=pl.ANY)
    operands = [gated, *weight] + ([partial] if other else [])
    shape = (width, cols) if other else (cols, width)
    return pl.pallas_call(
        lambda *refs: project_kernel(other, *refs),
        in_specs=[pl.BlockSpec(memory_space=pltpu.SMEM)] + [anywhere] * len(operands),
        out_specs=anywhere,
        out_shape=jax.ShapeDtypeStruct(shape, BF16 if other else F32),
        scratch_shapes=[
            pltpu.VMEM(gated.shape, BF16),
            pltpu.VMEM((depth, width), BF16),
            pltpu.VMEM((cols, depth), BF16),
            pltpu.VMEM(shape, BF16) if other else pltpu.VMEM((width // 256, cols, 256), F32),
        ]
        + ([pltpu.VMEM((cols, width), F32)] if other else [])
        + [pltpu.SemaphoreType.DMA((18 + width // 256,))],
        compiler_params=pltpu.CompilerParams(vmem_limit_bytes=VMEM_LIMIT - 0 * MIB),
        cost_estimate=pl.CostEstimate(flops=2 * depth * width * cols, bytes_accessed=2 * depth * width, transcendentals=0),
        name="project_last" if other else "project_first",
    )(place, *operands)


def turned(value, axis, steps):
    count = lax.axis_size(axis)
    return lax.ppermute(value, axis, [(source, (source + steps) % count) for source in range(count)])


def shards(query_proj, key_proj, value_proj, short_taps, long_filter, skip_bias, out_weight):
    rows, cols = query_proj.shape
    ctx = lax.axis_size(CTX)
    chans = long_filter.shape[0]
    tables = dft_tables(ctx, cols)

    taps = jnp.swapaxes(short_taps, 1, 2)
    place = jnp.stack([lax.axis_index(name) for name in (CTX, "zl", "zh", "core", "y", "x")]).astype(jnp.int32)

    pieces = [turned(out_weight, "zl", step) for step in (1, 2, 3)]
    ready = short_filters(taps, query_proj, key_proj, value_proj, ctx)
    ready, *pieces = lax.optimization_barrier((ready, *pieces))
    arrived = lax.all_to_all(ready, CTX, split_axis=0, concat_axis=0, tiled=True)

    first_half = jnp.concatenate([out_weight, pieces[0]], axis=0)
    second_half = jnp.concatenate(pieces[1:], axis=0)
    run_x = jnp.concatenate([first_half] + [turned(first_half, "x", step) for step in (1, 2, 3)], axis=0)
    run_y = jnp.concatenate([second_half] + [turned(second_half, "y", step) for step in (1, 2, 3)], axis=0)
    near = [turned(run_x, "y", 1), turned(run_x, "y", 3), turned(run_y, "x", 1), turned(run_y, "x", 3)]

    long_filter, run_x, run_y = lax.optimization_barrier((long_filter, run_x, run_y))
    spectrum = filter_spectrum(long_filter, tables, ctx, cols)
    gated = long_mix(place, arrived, spectrum, skip_bias, taps, tables, 2)
    gated, run_x, run_y, *near = lax.optimization_barrier((gated, run_x, run_y, *near))
    by_y = [run_x, near[0], turned(run_x, "y", 2), near[1]]
    by_x = [run_y, near[2], turned(run_y, "x", 2), near[3]]
    weight = by_y + by_x

    own = lax.all_to_all(
        gated.reshape(2 * ctx, chans, cols), CTX + ("zh",), split_axis=0, concat_axis=0, tiled=True
    ).reshape(ctx, 2, chans, cols)
    other = turned(own, "core", 1)
    return project(place, other, weight, project(place, own, weight))


def solution(mesh):
    fine = Mesh(mesh.devices.reshape(4, 4, 4, 2, 2), ("y", "x", "zl", "zh", "core"))
    mp = ("zh", "core")
    return jax.shard_map(
        shards,
        mesh=fine,
        in_specs=(
            P(mp, CTX),
            P(mp, CTX),
            P(mp, CTX),
            P(None, mp, None),
            P(mp + CTX, None),
            P(mp + CTX),
            P(CTX, mp),
        ),
        out_specs=P(mp, CTX),
        check_vma=False,
    )
```

```python
import math

import jax
import jax.numpy as jnp
import numpy as np
from jax import lax
from jax.experimental import pallas as pl
from jax.experimental.pallas import tpu as pltpu
from jax.sharding import Mesh, PartitionSpec as P

BF16 = jnp.bfloat16
F32 = jnp.float32
CTX = ("y", "x", "zl")
MIB = 1024 * 1024
VMEM_LIMIT = 60 * MIB


def hi_lo(table):
    hi = table.astype(np.float32).astype(jnp.bfloat16)
    lo = (table - hi.astype(np.float64)).astype(np.float32).astype(jnp.bfloat16)
    return hi, lo


def dft_tables(outer, inner):
    length = outer * inner
    freq = np.arange(outer)[:, None] + 0.25
    angle = 2.0 * np.pi * freq * np.arange(outer)[None, :] / outer
    first = np.concatenate([np.cos(angle), -np.sin(angle)], axis=0)
    spin = 2.0 * np.pi * freq * np.arange(inner)[None, :] / length
    steps = np.outer(np.arange(inner), np.arange(inner)) % inner
    turn = 2.0 * np.pi * steps / inner
    cos, sin = np.cos(turn), np.sin(turn)
    second = np.block([[cos, -sin], [sin, cos]])
    return {
        "first": hi_lo(first),
        "last": hi_lo(first.T.copy()),
        "spin": (np.cos(spin).astype(np.float32), np.sin(spin).astype(np.float32)),
        "second": hi_lo(second),
    }


def dot(left, right):
    return jnp.dot(left, right, preferred_element_type=F32)


def split_bf16(value):
    hi = value.astype(BF16)
    return hi, (value - hi.astype(F32)).astype(BF16)


def lane_ids(rows):
    return lax.broadcasted_iota(jnp.int32, (rows, 128), 1)


def filter_tiles(weights, before, tiles, lane):
    turned = {}
    for tap in range(1, len(weights)):
        for index, tile in enumerate(tiles):
            turned[index, tap] = pltpu.roll(tile, tap, 1)
        turned[-1, tap] = 0.0 if before is None else pltpu.roll(before, tap, 1)
    sums = []
    for index, tile in enumerate(tiles):
        total = weights[0] * tile
        for tap in range(1, len(weights)):
            total += weights[tap] * jnp.where(lane >= tap, turned[index, tap], turned[index - 1, tap])
        sums.append(total)
    return sums


def short_kernel(taps_ref, q_ref, k_ref, v_ref, out_ref):
    rows, cols = q_ref.shape
    taps = taps_ref.shape[1]
    size = out_ref.shape[1]
    first = pl.program_id(0) * (rows // size)
    lane = lane_ids(size)
    for g in range(rows // size):
        at = pl.ds(g * size, size)
        feats, edges = [], []
        for index, ref in ((1, k_ref), (2, v_ref)):
            wide = ref[at, :].astype(F32)
            tiles = [wide[:, i * 128 : i * 128 + 128] for i in range(cols // 128)]
            weights = [taps_ref[index, tap, first + g] for tap in range(taps)]
            feats.append(filter_tiles(weights, None, tiles, lane))
            shift = 8 if index == 1 else 24
            edges += [pltpu.roll(tiles[-1], shift, 1), pltpu.roll(tiles[0], shift, 1)]
        for i in range(cols // 128):
            out_ref[g, :, i * 128 : i * 128 + 128] = (feats[0][i] * feats[1][i]).astype(BF16)
        out_ref[g, :, cols : 2 * cols] = q_ref[at, :]
        edge = jnp.where(lane < 16, jnp.where(lane < 8, edges[0], edges[1]), jnp.where(lane < 24, edges[2], edges[3]))
        out_ref[g, :, 2 * cols :] = edge.astype(BF16)


def short_filters(taps, query, key, value, ctx, blocks=4):
    rows, cols = query.shape
    size = rows // ctx
    spec = pl.BlockSpec((rows // blocks, cols), lambda i: (i, 0))
    return pl.pallas_call(
        short_kernel,
        grid=(blocks,),
        in_specs=[pl.BlockSpec(memory_space=pltpu.SMEM)] + [spec] * 3,
        out_specs=pl.BlockSpec((ctx // blocks, size, 2 * cols + 128), lambda i: (i, 0, 0)),
        out_shape=jax.ShapeDtypeStruct((ctx, size, 2 * cols + 128), BF16),
        compiler_params=pltpu.CompilerParams(vmem_limit_bytes=VMEM_LIMIT),
        cost_estimate=pl.CostEstimate(flops=2 * 14 * rows * cols, bytes_accessed=10 * rows * cols, transcendentals=0),
        name="short_filters",
    )(taps, query, key, value)


def second_dft(hi, lo, second_hi, second_lo):
    return dot(hi, second_hi[...]) + dot(lo, second_hi[...]) + dot(hi, second_lo[...])


def channel_rows(ref, c, outer, chans):
    halves = ref.shape[0] // (outer * chans)
    parts = [ref[pl.ds(half * outer * chans + c, outer, stride=chans), :] for half in range(halves)]
    return jnp.concatenate(parts, axis=1)


def filter_kernel(scale, filt_ref, f_hi, f_lo, cos_ref, sin_ref, s_hi, s_lo, out_ref, rows_ref, g_hi, g_lo):
    chans, _ = filt_ref.shape
    outer, inner = cos_ref.shape
    for half in range(inner // 128):
        for a in range(outer):
            start = a * inner + half * 128
            at = (half * outer + a) * chans
            rows_ref[at : at + chans, :] = filt_ref[:, start : start + 128]

    for c in range(chans):
        hi, lo = split_bf16(channel_rows(rows_ref, c, outer, chans) * scale)
        mixed = dot(f_hi[...], hi) + dot(f_hi[...], lo) + dot(f_lo[...], hi)
        re, im = mixed[:outer], mixed[outer:]
        at = pl.ds(c * outer, outer)
        g_hi[at, :inner], g_lo[at, :inner] = split_bf16(re * cos_ref[...] + im * sin_ref[...])
        g_hi[at, inner:], g_lo[at, inner:] = split_bf16(im * cos_ref[...] - re * sin_ref[...])

    for i in range(chans * outer // 256):
        at = pl.ds(i * 256, 256)
        out_ref[at, :] = second_dft(g_hi[at, :], g_lo[at, :], s_hi, s_lo)


def filter_spectrum(long_filter, tables, outer, inner):
    chans = long_filter.shape[0]
    rows = chans * outer
    whole = lambda shape: pl.BlockSpec(shape, lambda i: (0,) * len(shape))
    operands = (long_filter, *tables["first"], *tables["spin"], *tables["second"])
    return pl.pallas_call(
        lambda *refs: filter_kernel(1.0 / (outer * inner), *refs),
        grid=(1,),
        in_specs=[whole(operand.shape) for operand in operands],
        out_specs=whole((rows, 2 * inner)),
        out_shape=jax.ShapeDtypeStruct((rows, 2 * inner), F32),
        scratch_shapes=[
            pltpu.VMEM((rows * inner // 128, 128), F32),
            pltpu.VMEM((rows, 2 * inner), BF16),
            pltpu.VMEM((rows, 2 * inner), BF16),
        ],
        compiler_params=pltpu.CompilerParams(vmem_limit_bytes=VMEM_LIMIT),
        cost_estimate=pl.CostEstimate(flops=3 * 2 * rows * 4 * inner * inner, bytes_accessed=5 * 2**20, transcendentals=0),
        name="filter_spectrum",
    )(*operands)


def conv_kernel(
    place_ref, skip_ref, taps_ref, in_ref, f_hi, f_lo, l_hi, l_lo, cos_ref, sin_ref, spec_hbm, s_hi_hbm, s_lo_hbm,
    out_ref, rows_ref, z_ref, q_ref, edge_ref, g_hi, g_lo, spec_ref, s_hi, s_lo, sems,
):
    fetches = [
        pltpu.make_async_copy(source, target, sems.at[index])
        for index, (source, target) in enumerate(((spec_hbm, spec_ref), (s_hi_hbm, s_hi), (s_lo_hbm, s_lo)))
    ]
    for fetch in fetches:
        fetch.start()
    outer, chans, width = in_ref.shape
    inner = (width - 128) // 2
    halves = inner // 128
    rows = outer * chans
    taps = taps_ref.shape[1]
    group = place_ref[0]
    blocks = 8
    step = rows // blocks
    units = outer // blocks
    lane = lane_ids(step)

    edge_ref[:chans, :] = jnp.zeros((chans, 128), F32)
    q_ref[(halves - 1) * (rows + chans) : (halves - 1) * (rows + chans) + chans, :] = jnp.zeros((chans, 128), F32)
    edge_ref[chans:, :] = in_ref[:, :, 2 * inner :].reshape(rows, 128).astype(F32)
    for half in range(halves):
        at = half * (rows + chans) + chans
        q_ref[at : at + rows, :] = (
            in_ref[:, :, inner + half * 128 : inner + half * 128 + 128].reshape(rows, 128).astype(F32)
        )

    weights = [jnp.where(lane < 16, taps_ref[1, tap, group], taps_ref[2, tap, group]) for tap in range(taps)]

    for i in range(blocks):
        at = i * step
        edge = jnp.where(jnp.bitwise_and(lane, 8) == 0, edge_ref[at : at + step, :], edge_ref[at + chans : at + chans + step, :])
        total = weights[0] * edge
        for tap in range(1, taps):
            total += weights[tap] * pltpu.roll(edge, tap, 1)
        first = (pltpu.roll(total, 120, 1) * pltpu.roll(total, 104, 1)).astype(BF16).astype(F32)
        sig = in_ref[i * units : (i + 1) * units, :, :inner].reshape(step, inner).astype(F32)
        rows_ref[at : at + step, :] = jnp.where(lane < taps - 1, first, sig[:, :128])
        for half in range(1, halves):
            rows_ref[half * rows + at : half * rows + at + step, :] = sig[:, half * 128 : half * 128 + 128]

    for c in range(chans):
        sig = channel_rows(rows_ref, c, outer, chans).astype(BF16)
        mixed = dot(f_hi[...], sig) + dot(f_lo[...], sig)
        re, im = mixed[:outer], mixed[outer:]
        at = pl.ds(c * outer, outer)
        g_hi[at, :inner], g_lo[at, :inner] = split_bf16(re * cos_ref[...] + im * sin_ref[...])
        g_hi[at, inner:], g_lo[at, inner:] = split_bf16(im * cos_ref[...] - re * sin_ref[...])

    for fetch in fetches:
        fetch.wait()

    block = min(chans * outer, 512)
    for i in range(chans * outer // block):
        at = pl.ds(i * block, block)
        sig = second_dft(g_hi[at, :], g_lo[at, :], s_hi, s_lo)
        sr, si = sig[:, :inner], sig[:, inner:]
        hr, hm = spec_ref[at, :inner], spec_ref[at, inner:]
        r_hi, r_lo = split_bf16(sr * hr - si * hm)
        i_hi, i_lo = split_bf16(-(sr * hm + si * hr))
        back = second_dft(
            jnp.concatenate([r_hi, i_hi], axis=1), jnp.concatenate([r_lo, i_lo], axis=1), s_hi, s_lo
        )
        back = back.reshape(block // outer, outer, 2 * inner)
        re, im = back[:, :, :inner], back[:, :, inner:]
        cos, sin = cos_ref[...], sin_ref[...]
        r_hi, r_lo = split_bf16((re * cos + im * sin).reshape(block, inner))
        i_hi, i_lo = split_bf16((re * sin - im * cos).reshape(block, inner))
        for j in range(block // outer):
            c = i * (block // outer) + j
            part = slice(j * outer, (j + 1) * outer)
            hi = jnp.concatenate([r_hi[part], i_hi[part]], axis=0)
            lo = jnp.concatenate([r_lo[part], i_lo[part]], axis=0)
            conv = dot(l_hi[...], hi) + dot(l_hi[...], lo) + dot(l_lo[...], hi)
            mixed = conv + skip_ref[c] * channel_rows(rows_ref, c, outer, chans)
            for half in range(halves):
                z_ref[pl.ds(half * rows + c, outer, stride=chans), :] = mixed[:, half * 128 : (half + 1) * 128]

    q_taps = [taps_ref[0, tap, group] for tap in range(taps)]
    for i in range(blocks):
        at = i * step
        starts = [half * (rows + chans) + chans + at for half in range(halves)]
        tiles = [q_ref[start : start + step, :] for start in starts]
        start = (halves - 1) * (rows + chans) + at
        feats = filter_tiles(q_taps, q_ref[start : start + step, :], tiles, lane)
        for half in range(halves):
            mixed = z_ref[half * rows + at : half * rows + at + step, :].astype(BF16).astype(F32)
            result = (feats[half] * mixed).astype(BF16).reshape(units, chans, 128)
            for copy in range(out_ref.shape[1]):
                out_ref[i * units : (i + 1) * units, copy, :, half * 128 : (half + 1) * 128] = result


def long_mix(place, arrived, spectrum, skip_bias, taps, tables, copies):
    outer, chans, width = arrived.shape
    inner = (width - 128) // 2
    rows = outer * chans
    whole = lambda shape: pl.BlockSpec(shape, lambda i: (0,) * len(shape))
    scalars = pl.BlockSpec(memory_space=pltpu.SMEM)
    operands = (arrived, *tables["first"], *tables["last"], *tables["spin"])
    fetched = (spectrum, *tables["second"])
    return pl.pallas_call(
        conv_kernel,
        grid=(1,),
        in_specs=[scalars] * 3
        + [whole(operand.shape) for operand in operands]
        + [pl.BlockSpec(memory_space=pl.ANY)] * len(fetched),
        out_specs=whole((outer, copies, chans, inner)),
        out_shape=jax.ShapeDtypeStruct((outer, copies, chans, inner), BF16),
        scratch_shapes=[
            pltpu.VMEM((rows * inner // 128, 128), F32),
            pltpu.VMEM((rows * inner // 128, 128), F32),
            pltpu.VMEM(((rows + chans) * inner // 128, 128), F32),
            pltpu.VMEM((rows + chans, 128), F32),
            pltpu.VMEM((rows, 2 * inner), BF16),
            pltpu.VMEM((rows, 2 * inner), BF16),
            pltpu.VMEM((rows, 2 * inner), F32),
            pltpu.VMEM((2 * inner, 2 * inner), BF16),
            pltpu.VMEM((2 * inner, 2 * inner), BF16),
            pltpu.SemaphoreType.DMA((3,)),
        ],
        compiler_params=pltpu.CompilerParams(vmem_limit_bytes=VMEM_LIMIT - 10 * MIB),
        cost_estimate=pl.CostEstimate(flops=2**20, bytes_accessed=2**20, transcendentals=0),
        name="long_conv",
    )(place, skip_bias, taps, *operands, *fetched)


def project_kernel(other, place_ref, z_hbm, *refs):
    if other:
        w_hbm, sum_hbm, out_hbm, z_ref, w_ref, g_ref, out_ref, sum_ref, sems = refs
    else:
        w_hbm, out_hbm, z_ref, w_ref, g_ref, out_ref, sems = refs
    _, halves, chans, cols = z_ref.shape
    depth, width = w_ref.shape
    unit = 4 * chans
    size = 4 * unit
    block = 256
    zl = place_ref[1]
    core = jnp.bitwise_xor(place_ref[3], other)

    def copy(source, target, index):
        fetch = pltpu.make_async_copy(source, target, sems.at[index])
        fetch.start()
        return fetch

    arriving = copy(z_hbm, z_ref, 0)
    fetches = []
    for half in range(halves):
        for x in range(4):
            index = half * 4 + x
            start = pl.multiple_of(((half * 2 + core) * 4 + x) * size, size)
            fetches.append(copy(w_hbm.at[pl.ds(start, size)], w_ref.at[pl.ds(index * size, size)], 1 + index))
    if other:
        fetches.append(copy(sum_hbm, sum_ref, 9))
    arriving.wait()
    for half in range(halves):
        for x in range(4):
            parts = []
            for turn in range(4):
                start = x * 16 + 4 * jnp.bitwise_and(zl - turn, 3)
                parts.append(z_ref[pl.ds(start, 4), half].reshape(unit, cols))
            to = (half * 4 + x) * size
            g_ref[:, to : to + size] = jnp.concatenate(parts, axis=0).T
    held = sum_ref if other else out_ref
    middle = depth // 2
    for fetch in fetches[:4] + fetches[8:]:
        fetch.wait()
    for index in range(width // block):
        at = slice(index * block, (index + 1) * block)
        part = dot(g_ref[:, :middle], w_ref[:middle, at])
        if other:
            held[:, at] += part
        else:
            held[index] = part
    for fetch in fetches[4:8]:
        fetch.wait()
    leaving = []
    for index in range(width // block):
        at = slice(index * block, (index + 1) * block)
        part = dot(g_ref[:, middle:], w_ref[middle:, at])
        if other:
            out_ref[at, :] = (part + held[:, at]).T.astype(BF16)
            leaving.append(copy(out_ref.at[at], out_hbm.at[at], 10 + index))
        else:
            held[index] += part
            leaving.append(copy(out_ref.at[index], out_hbm.at[:, at], 10 + index))
    for leave in leaving:
        leave.wait()


def project(place, gated, weight, partial=None):
    width = weight.shape[1]
    depth = weight.shape[0] // 2
    cols = gated.shape[3]
    other = 0 if partial is None else 1
    anywhere = pl.BlockSpec(memory_space=pl.ANY)
    operands = [gated, weight] + ([partial] if other else [])
    shape = (width, cols) if other else (cols, width)
    return pl.pallas_call(
        lambda *refs: project_kernel(other, *refs),
        in_specs=[pl.BlockSpec(memory_space=pltpu.SMEM)] + [anywhere] * len(operands),
        out_specs=anywhere,
        out_shape=jax.ShapeDtypeStruct(shape, BF16 if other else F32),
        scratch_shapes=[
            pltpu.VMEM(gated.shape, BF16),
            pltpu.VMEM((depth, width), BF16),
            pltpu.VMEM((cols, depth), BF16),
            pltpu.VMEM(shape, BF16) if other else pltpu.VMEM((width // 256, cols, 256), F32),
        ]
        + ([pltpu.VMEM((cols, width), F32)] if other else [])
        + [pltpu.SemaphoreType.DMA((10 + width // 256,))],
        compiler_params=pltpu.CompilerParams(vmem_limit_bytes=VMEM_LIMIT - 12 * MIB),
        cost_estimate=pl.CostEstimate(flops=2 * depth * width * cols, bytes_accessed=2 * depth * width, transcendentals=0),
        name="project_last" if other else "project_first",
    )(place, *operands)


def turned(value, axis, steps):
    count = lax.axis_size(axis)
    return lax.ppermute(value, axis, [(source, (source + steps) % count) for source in range(count)])


def shards(query_proj, key_proj, value_proj, short_taps, long_filter, skip_bias, out_weight):
    rows, cols = query_proj.shape
    ctx = lax.axis_size(CTX)
    chans = long_filter.shape[0]
    tables = dft_tables(ctx, cols)

    taps = jnp.swapaxes(short_taps, 1, 2)
    place = jnp.stack([lax.axis_index(name) for name in (CTX, "zl", "zh", "core")]).astype(jnp.int32)

    pieces = [turned(out_weight, "zl", step) for step in (1, 2, 3)]
    ready = short_filters(taps, query_proj, key_proj, value_proj, ctx)
    ready, *pieces = lax.optimization_barrier((ready, *pieces))
    weight = lax.all_gather(jnp.concatenate([out_weight, *pieces], axis=0), ("y", "x"), axis=0, tiled=True)

    spectrum = filter_spectrum(long_filter, tables, ctx, cols)
    arrived = lax.all_to_all(ready, CTX, split_axis=0, concat_axis=0, tiled=True)
    gated = long_mix(place, arrived, spectrum, skip_bias, taps, tables, 2)
    own = lax.all_to_all(
        gated.reshape(2 * ctx, chans, cols), CTX + ("zh",), split_axis=0, concat_axis=0, tiled=True
    ).reshape(ctx, 2, chans, cols)
    other = turned(own, "core", 1)
    return project(place, other, weight, project(place, own, weight))


def solution(mesh):
    fine = Mesh(mesh.devices.reshape(4, 4, 4, 2, 2), ("y", "x", "zl", "zh", "core"))
    mp = ("zh", "core")
    return jax.shard_map(
        shards,
        mesh=fine,
        in_specs=(
            P(mp, CTX),
            P(mp, CTX),
            P(mp, CTX),
            P(None, mp, None),
            P(mp + CTX, None),
            P(mp + CTX),
            P(CTX, mp),
        ),
        out_specs=P(mp, CTX),
        check_vma=False,
    )
```

```python
import math

import jax
import jax.numpy as jnp
import numpy as np
from jax import lax
from jax.experimental import pallas as pl
from jax.experimental.pallas import tpu as pltpu
from jax.sharding import Mesh, PartitionSpec as P

BF16 = jnp.bfloat16
F32 = jnp.float32
CTX = ("y", "x", "zl")
MIB = 1024 * 1024
VMEM_LIMIT = 60 * MIB


def hi_lo(table):
    hi = table.astype(np.float32).astype(jnp.bfloat16)
    lo = (table - hi.astype(np.float64)).astype(np.float32).astype(jnp.bfloat16)
    return hi, lo


def dft_tables(outer, inner):
    length = outer * inner
    freq = np.arange(outer)[:, None] + 0.25
    angle = 2.0 * np.pi * freq * np.arange(outer)[None, :] / outer
    first = np.concatenate([np.cos(angle), -np.sin(angle)], axis=0)
    spin = 2.0 * np.pi * freq * np.arange(inner)[None, :] / length
    steps = np.outer(np.arange(inner), np.arange(inner)) % inner
    turn = 2.0 * np.pi * steps / inner
    cos, sin = np.cos(turn), np.sin(turn)
    second = np.block([[cos, -sin], [sin, cos]])
    return {
        "first": hi_lo(first),
        "last": hi_lo(first.T.copy()),
        "spin": (np.cos(spin).astype(np.float32), np.sin(spin).astype(np.float32)),
        "second": hi_lo(second),
    }


def dot(left, right):
    return jnp.dot(left, right, preferred_element_type=F32)


def split_bf16(value):
    hi = value.astype(BF16)
    return hi, (value - hi.astype(F32)).astype(BF16)


def lane_ids(rows):
    return lax.broadcasted_iota(jnp.int32, (rows, 128), 1)


def filter_tiles(weights, before, tiles, lane):
    turned = {}
    for tap in range(1, len(weights)):
        for index, tile in enumerate(tiles):
            turned[index, tap] = pltpu.roll(tile, tap, 1)
        turned[-1, tap] = 0.0 if before is None else pltpu.roll(before, tap, 1)
    sums = []
    for index, tile in enumerate(tiles):
        total = weights[0] * tile
        for tap in range(1, len(weights)):
            total += weights[tap] * jnp.where(lane >= tap, turned[index, tap], turned[index - 1, tap])
        sums.append(total)
    return sums


def short_kernel(taps_ref, q_ref, k_ref, v_ref, out_ref):
    rows, cols = q_ref.shape
    taps = taps_ref.shape[1]
    size = out_ref.shape[1]
    first = pl.program_id(0) * (rows // size)
    lane = lane_ids(size)
    for g in range(rows // size):
        at = pl.ds(g * size, size)
        feats, edges = [], []
        for index, ref in ((1, k_ref), (2, v_ref)):
            wide = ref[at, :].astype(F32)
            tiles = [wide[:, i * 128 : i * 128 + 128] for i in range(cols // 128)]
            weights = [taps_ref[index, tap, first + g] for tap in range(taps)]
            feats.append(filter_tiles(weights, None, tiles, lane))
            shift = 8 if index == 1 else 24
            edges += [pltpu.roll(tiles[-1], shift, 1), pltpu.roll(tiles[0], shift, 1)]
        for i in range(cols // 128):
            out_ref[g, :, i * 128 : i * 128 + 128] = (feats[0][i] * feats[1][i]).astype(BF16)
        out_ref[g, :, cols : 2 * cols] = q_ref[at, :]
        edge = jnp.where(lane < 16, jnp.where(lane < 8, edges[0], edges[1]), jnp.where(lane < 24, edges[2], edges[3]))
        out_ref[g, :, 2 * cols :] = edge.astype(BF16)


def short_filters(taps, query, key, value, ctx, blocks=4):
    rows, cols = query.shape
    size = rows // ctx
    spec = pl.BlockSpec((rows // blocks, cols), lambda i: (i, 0))
    return pl.pallas_call(
        short_kernel,
        grid=(blocks,),
        in_specs=[pl.BlockSpec(memory_space=pltpu.SMEM)] + [spec] * 3,
        out_specs=pl.BlockSpec((ctx // blocks, size, 2 * cols + 128), lambda i: (i, 0, 0)),
        out_shape=jax.ShapeDtypeStruct((ctx, size, 2 * cols + 128), BF16),
        compiler_params=pltpu.CompilerParams(vmem_limit_bytes=VMEM_LIMIT),
        cost_estimate=pl.CostEstimate(flops=2 * 14 * rows * cols, bytes_accessed=10 * rows * cols, transcendentals=0),
        name="short_filters",
    )(taps, query, key, value)


def second_dft(hi, lo, second_hi, second_lo):
    return dot(hi, second_hi[...]) + dot(lo, second_hi[...]) + dot(hi, second_lo[...])


def channel_rows(ref, c, outer, chans):
    halves = ref.shape[0] // (outer * chans)
    parts = [ref[pl.ds(half * outer * chans + c, outer, stride=chans), :] for half in range(halves)]
    return jnp.concatenate(parts, axis=1)


def filter_kernel(scale, filt_ref, f_hi, f_lo, cos_ref, sin_ref, s_hi, s_lo, out_ref, rows_ref, g_hi, g_lo):
    chans, _ = filt_ref.shape
    outer, inner = cos_ref.shape
    for half in range(inner // 128):
        for a in range(outer):
            start = a * inner + half * 128
            at = (half * outer + a) * chans
            rows_ref[at : at + chans, :] = filt_ref[:, start : start + 128]

    for c in range(chans):
        hi, lo = split_bf16(channel_rows(rows_ref, c, outer, chans) * scale)
        mixed = dot(f_hi[...], hi) + dot(f_hi[...], lo) + dot(f_lo[...], hi)
        re, im = mixed[:outer], mixed[outer:]
        at = pl.ds(c * outer, outer)
        g_hi[at, :inner], g_lo[at, :inner] = split_bf16(re * cos_ref[...] + im * sin_ref[...])
        g_hi[at, inner:], g_lo[at, inner:] = split_bf16(im * cos_ref[...] - re * sin_ref[...])

    for i in range(chans * outer // 256):
        at = pl.ds(i * 256, 256)
        out_ref[at, :] = second_dft(g_hi[at, :], g_lo[at, :], s_hi, s_lo)


def filter_spectrum(long_filter, tables, outer, inner):
    chans = long_filter.shape[0]
    rows = chans * outer
    whole = lambda shape: pl.BlockSpec(shape, lambda i: (0,) * len(shape))
    operands = (long_filter, *tables["first"], *tables["spin"], *tables["second"])
    return pl.pallas_call(
        lambda *refs: filter_kernel(1.0 / (outer * inner), *refs),
        grid=(1,),
        in_specs=[whole(operand.shape) for operand in operands],
        out_specs=whole((rows, 2 * inner)),
        out_shape=jax.ShapeDtypeStruct((rows, 2 * inner), F32),
        scratch_shapes=[
            pltpu.VMEM((rows * inner // 128, 128), F32),
            pltpu.VMEM((rows, 2 * inner), BF16),
            pltpu.VMEM((rows, 2 * inner), BF16),
        ],
        compiler_params=pltpu.CompilerParams(vmem_limit_bytes=VMEM_LIMIT),
        cost_estimate=pl.CostEstimate(flops=3 * 2 * rows * 4 * inner * inner, bytes_accessed=5 * 2**20, transcendentals=0),
        name="filter_spectrum",
    )(*operands)


def conv_kernel(
    place_ref, skip_ref, taps_ref, in_ref, f_hi, f_lo, l_hi, l_lo, cos_ref, sin_ref, spec_hbm, s_hi_hbm, s_lo_hbm,
    out_ref, rows_ref, z_ref, q_ref, edge_ref, g_hi, g_lo, spec_ref, s_hi, s_lo, sems,
):
    fetches = [
        pltpu.make_async_copy(source, target, sems.at[index])
        for index, (source, target) in enumerate(((spec_hbm, spec_ref), (s_hi_hbm, s_hi), (s_lo_hbm, s_lo)))
    ]
    for fetch in fetches:
        fetch.start()
    outer, chans, width = in_ref.shape
    inner = (width - 128) // 2
    halves = inner // 128
    rows = outer * chans
    taps = taps_ref.shape[1]
    group = place_ref[0]
    blocks = 8
    step = rows // blocks
    units = outer // blocks
    lane = lane_ids(step)

    edge_ref[:chans, :] = jnp.zeros((chans, 128), F32)
    q_ref[(halves - 1) * (rows + chans) : (halves - 1) * (rows + chans) + chans, :] = jnp.zeros((chans, 128), F32)
    edge_ref[chans:, :] = in_ref[:, :, 2 * inner :].reshape(rows, 128).astype(F32)
    for half in range(halves):
        at = half * (rows + chans) + chans
        q_ref[at : at + rows, :] = (
            in_ref[:, :, inner + half * 128 : inner + half * 128 + 128].reshape(rows, 128).astype(F32)
        )

    weights = [jnp.where(lane < 16, taps_ref[1, tap, group], taps_ref[2, tap, group]) for tap in range(taps)]

    for i in range(blocks):
        at = i * step
        edge = jnp.where(jnp.bitwise_and(lane, 8) == 0, edge_ref[at : at + step, :], edge_ref[at + chans : at + chans + step, :])
        total = weights[0] * edge
        for tap in range(1, taps):
            total += weights[tap] * pltpu.roll(edge, tap, 1)
        first = (pltpu.roll(total, 120, 1) * pltpu.roll(total, 104, 1)).astype(BF16).astype(F32)
        sig = in_ref[i * units : (i + 1) * units, :, :inner].reshape(step, inner).astype(F32)
        rows_ref[at : at + step, :] = jnp.where(lane < taps - 1, first, sig[:, :128])
        for half in range(1, halves):
            rows_ref[half * rows + at : half * rows + at + step, :] = sig[:, half * 128 : half * 128 + 128]

    for c in range(chans):
        sig = channel_rows(rows_ref, c, outer, chans).astype(BF16)
        mixed = dot(f_hi[...], sig) + dot(f_lo[...], sig)
        re, im = mixed[:outer], mixed[outer:]
        at = pl.ds(c * outer, outer)
        g_hi[at, :inner], g_lo[at, :inner] = split_bf16(re * cos_ref[...] + im * sin_ref[...])
        g_hi[at, inner:], g_lo[at, inner:] = split_bf16(im * cos_ref[...] - re * sin_ref[...])

    for fetch in fetches:
        fetch.wait()

    block = min(chans * outer, 512)
    for i in range(chans * outer // block):
        at = pl.ds(i * block, block)
        sig = second_dft(g_hi[at, :], g_lo[at, :], s_hi, s_lo)
        sr, si = sig[:, :inner], sig[:, inner:]
        hr, hm = spec_ref[at, :inner], spec_ref[at, inner:]
        r_hi, r_lo = split_bf16(sr * hr - si * hm)
        i_hi, i_lo = split_bf16(-(sr * hm + si * hr))
        back = second_dft(
            jnp.concatenate([r_hi, i_hi], axis=1), jnp.concatenate([r_lo, i_lo], axis=1), s_hi, s_lo
        )
        back = back.reshape(block // outer, outer, 2 * inner)
        re, im = back[:, :, :inner], back[:, :, inner:]
        cos, sin = cos_ref[...], sin_ref[...]
        r_hi, r_lo = split_bf16((re * cos + im * sin).reshape(block, inner))
        i_hi, i_lo = split_bf16((re * sin - im * cos).reshape(block, inner))
        for j in range(block // outer):
            c = i * (block // outer) + j
            part = slice(j * outer, (j + 1) * outer)
            hi = jnp.concatenate([r_hi[part], i_hi[part]], axis=0)
            lo = jnp.concatenate([r_lo[part], i_lo[part]], axis=0)
            conv = dot(l_hi[...], hi) + dot(l_hi[...], lo) + dot(l_lo[...], hi)
            mixed = conv + skip_ref[c] * channel_rows(rows_ref, c, outer, chans)
            for half in range(halves):
                z_ref[pl.ds(half * rows + c, outer, stride=chans), :] = mixed[:, half * 128 : (half + 1) * 128]

    q_taps = [taps_ref[0, tap, group] for tap in range(taps)]
    for i in range(blocks):
        at = i * step
        starts = [half * (rows + chans) + chans + at for half in range(halves)]
        tiles = [q_ref[start : start + step, :] for start in starts]
        start = (halves - 1) * (rows + chans) + at
        feats = filter_tiles(q_taps, q_ref[start : start + step, :], tiles, lane)
        for half in range(halves):
            mixed = z_ref[half * rows + at : half * rows + at + step, :].astype(BF16).astype(F32)
            result = (feats[half] * mixed).astype(BF16).reshape(units, chans, 128)
            for copy in range(out_ref.shape[1]):
                out_ref[i * units : (i + 1) * units, copy, :, half * 128 : (half + 1) * 128] = result


def long_mix(place, arrived, spectrum, skip_bias, taps, tables, copies):
    outer, chans, width = arrived.shape
    inner = (width - 128) // 2
    rows = outer * chans
    whole = lambda shape: pl.BlockSpec(shape, lambda i: (0,) * len(shape))
    scalars = pl.BlockSpec(memory_space=pltpu.SMEM)
    operands = (arrived, *tables["first"], *tables["last"], *tables["spin"])
    fetched = (spectrum, *tables["second"])
    return pl.pallas_call(
        conv_kernel,
        grid=(1,),
        in_specs=[scalars] * 3
        + [whole(operand.shape) for operand in operands]
        + [pl.BlockSpec(memory_space=pl.ANY)] * len(fetched),
        out_specs=whole((outer, copies, chans, inner)),
        out_shape=jax.ShapeDtypeStruct((outer, copies, chans, inner), BF16),
        scratch_shapes=[
            pltpu.VMEM((rows * inner // 128, 128), F32),
            pltpu.VMEM((rows * inner // 128, 128), F32),
            pltpu.VMEM(((rows + chans) * inner // 128, 128), F32),
            pltpu.VMEM((rows + chans, 128), F32),
            pltpu.VMEM((rows, 2 * inner), BF16),
            pltpu.VMEM((rows, 2 * inner), BF16),
            pltpu.VMEM((rows, 2 * inner), F32),
            pltpu.VMEM((2 * inner, 2 * inner), BF16),
            pltpu.VMEM((2 * inner, 2 * inner), BF16),
            pltpu.SemaphoreType.DMA((3,)),
        ],
        compiler_params=pltpu.CompilerParams(vmem_limit_bytes=VMEM_LIMIT - 10 * MIB),
        cost_estimate=pl.CostEstimate(flops=2**20, bytes_accessed=2**20, transcendentals=0),
        name="long_conv",
    )(place, skip_bias, taps, *operands, *fetched)


def project_kernel(place_ref, own_hbm, other_hbm, w_hbm, out_hbm, z_ref, w_ref, g_ref, sum_ref, out_ref, sems):
    cores, _, halves, chans, cols = z_ref.shape
    depth, width = w_ref.shape
    unit = 4 * chans
    size = 4 * unit
    panel = 4 * size
    block = 256
    zl = place_ref[1]

    def copy(source, target, index):
        fetch = pltpu.make_async_copy(source, target, sems.at[index])
        fetch.start()
        return fetch

    arriving = [copy(own_hbm, z_ref.at[0], 0), copy(other_hbm, z_ref.at[1], 1)]
    fetches = []
    for other in range(cores):
        for half in range(halves):
            start = (half * 2 + jnp.bitwise_xor(place_ref[3], other)) * panel
            for x in range(4):
                index = (other * halves + half) * 4 + x
                source = pl.ds(pl.multiple_of(start + x * size, size), size)
                fetches.append(copy(w_hbm.at[source], w_ref.at[pl.ds(index * size, size)], 2 + index))
    leaving = []
    for other in range(cores):
        arriving[other].wait()
        for half in range(halves):
            base = (other * halves + half) * panel
            for x in range(4):
                parts = []
                for turn in range(4):
                    start = x * 16 + 4 * jnp.bitwise_and(zl - turn, 3)
                    parts.append(z_ref[other, pl.ds(start, 4), half].reshape(unit, cols))
                g_ref[:, base + x * size : base + (x + 1) * size] = jnp.concatenate(parts, axis=0).T
    for part in range(cores * halves):
        for fetch in fetches[part * 4 : part * 4 + 4]:
            fetch.wait()
        rows = slice(part * panel, (part + 1) * panel)
        for index in range(width // block):
            at = slice(index * block, (index + 1) * block)
            total = dot(g_ref[:, rows], w_ref[rows, at])
            if part:
                total += sum_ref[:, at]
            if part < cores * halves - 1:
                sum_ref[:, at] = total
            else:
                out_ref[at, :] = total.T.astype(BF16)
                leaving.append(copy(out_ref.at[at], out_hbm.at[at], 18 + index))
    for leave in leaving:
        leave.wait()


def project(place, own, other, weight):
    depth, width = weight.shape
    cols = own.shape[3]
    anywhere = pl.BlockSpec(memory_space=pl.ANY)
    return pl.pallas_call(
        project_kernel,
        in_specs=[pl.BlockSpec(memory_space=pltpu.SMEM)] + [anywhere] * 3,
        out_specs=anywhere,
        out_shape=jax.ShapeDtypeStruct((width, cols), BF16),
        scratch_shapes=[
            pltpu.VMEM((2, *own.shape), BF16),
            pltpu.VMEM((depth, width), BF16),
            pltpu.VMEM((cols, depth), BF16),
            pltpu.VMEM((cols, width), F32),
            pltpu.VMEM((width, cols), BF16),
            pltpu.SemaphoreType.DMA((18 + width // 256,)),
        ],
        compiler_params=pltpu.CompilerParams(vmem_limit_bytes=VMEM_LIMIT - 12 * MIB),
        cost_estimate=pl.CostEstimate(flops=2 * depth * width * cols, bytes_accessed=2 * depth * width, transcendentals=0),
        name="project",
    )(place, own, other, weight)


def turned(value, axis, steps):
    count = lax.axis_size(axis)
    return lax.ppermute(value, axis, [(source, (source + steps) % count) for source in range(count)])


def shards(query_proj, key_proj, value_proj, short_taps, long_filter, skip_bias, out_weight):
    rows, cols = query_proj.shape
    ctx = lax.axis_size(CTX)
    chans = long_filter.shape[0]
    tables = dft_tables(ctx, cols)

    taps = jnp.swapaxes(short_taps, 1, 2)
    place = jnp.stack([lax.axis_index(name) for name in (CTX, "zl", "zh", "core")]).astype(jnp.int32)

    pieces = [turned(out_weight, "zl", step) for step in (1, 2, 3)]
    ready = short_filters(taps, query_proj, key_proj, value_proj, ctx)
    ready, *pieces = lax.optimization_barrier((ready, *pieces))
    weight = lax.all_gather(jnp.concatenate([out_weight, *pieces], axis=0), ("y", "x"), axis=0, tiled=True)

    spectrum = filter_spectrum(long_filter, tables, ctx, cols)
    arrived = lax.all_to_all(ready, CTX, split_axis=0, concat_axis=0, tiled=True)
    gated = long_mix(place, arrived, spectrum, skip_bias, taps, tables, 2)
    own = lax.all_to_all(
        gated.reshape(2 * ctx, chans, cols), CTX + ("zh",), split_axis=0, concat_axis=0, tiled=True
    ).reshape(ctx, 2, chans, cols)
    other = turned(own, "core", 1)
    return project(place, own, other, weight)


def solution(mesh):
    fine = Mesh(mesh.devices.reshape(4, 4, 4, 2, 2), ("y", "x", "zl", "zh", "core"))
    mp = ("zh", "core")
    return jax.shard_map(
        shards,
        mesh=fine,
        in_specs=(
            P(mp, CTX),
            P(mp, CTX),
            P(mp, CTX),
            P(None, mp, None),
            P(mp + CTX, None),
            P(mp + CTX),
            P(CTX, mp),
        ),
        out_specs=P(mp, CTX),
        check_vma=False,
    )
```
